32 devices in a mesh: dp: 4 (over y, core), shard: 8 (over z, x).
Axes of the slice: x: 2, y: 2, z: 4, core: 2. Of those that a mesh axis runs over, the one named last changes fastest.
Arguments:
- tokens: bfloat16 [3072, 8, 1024], P('shard', 'dp'), may hold values from -6 to 6
- dino: bfloat16 [4096, 8, 768], P('shard', 'dp'), may hold values from -6 to 6
- first_gain: float32 [1024], P(('dp', 'shard')), may hold values from 0.1 to 1.9
- first_shift: float32 [1024], P(('dp', 'shard')), may hold values from -0.625 to 0.625
- image_weight: float32 [768, 1024], P(('dp', 'shard')), may hold values from -0.21875 to 0.21875
- cross_query: float32 [1024, 1024], P(('dp', 'shard')), may hold values from -0.1875 to 0.1875
- cross_keyval: float32 [1024, 2048], P(('dp', 'shard')), may hold values from -0.1875 to 0.1875
- cross_output: float32 [1024, 1024], P(('dp', 'shard')), may hold values from -6 to 6
- second_gain: float32 [1024], P(('dp', 'shard')), may hold values from 0.1 to 1.9
- second_shift: float32 [1024], P(('dp', 'shard')), may hold values from -0.125 to 0.125
- self_project: float32 [1024, 3072], P(('dp', 'shard')), may hold values from -0.1875 to 0.1875
- self_output: float32 [1024, 1024], P(('dp', 'shard')), may hold values from -6 to 6
- third_gain: float32 [1024], P(('dp', 'shard')), may hold values from 0.1 to 1.9
- third_shift: float32 [1024], P(('dp', 'shard')), may hold values from -0.625 to 0.625
- hidden_weight: float32 [1024, 4096], P(('dp', 'shard')), may hold values from -0.1875 to 0.1875
- hidden_bias: float32 [4096], P(('dp', 'shard')), may hold values from -1.75 to 1.75
- output_weight: float32 [4096, 1024], P(('dp', 'shard')), may hold values from -0.09375 to 0.09375
- deconv_weight: float32 [1024, 320], P(('dp', 'shard')), may hold values from -0.1875 to 0.1875
- ray_mask: int32 [8192], P(('dp', 'shard')), may hold values 0 or 1
- block_object: int32 [64], P(('dp', 'shard')), may hold values from 0 to 1
- sample_cell: int32 [3, 262144], P(None, ('dp', 'shard')), may hold values from 0 to 4030
- sample_frac: float32 [6, 262144], P(None, ('dp', 'shard')), may hold values from 0 to 1
- out_grad: bfloat16 [3072, 8, 1024], P('shard', 'dp'), may hold values from -8 to 8
- sampled_grad: bfloat16 [8192, 2560], P(('dp', 'shard')), may hold values from -6 to 6
Outputs:
- tokens_out: bfloat16 [3072, 8, 1024], P('shard', 'dp')
- sampled: bfloat16 [8192, 2560], P(('dp', 'shard'))
- tokens_grad: float32 [3072, 8, 1024], P('shard', 'dp')
- dino_grad: float32 [4096, 8, 768], P('shard', 'dp')
- first_gain_grad: float32 [1024], P(('dp', 'shard'))
- first_shift_grad: float32 [1024], P(('dp', 'shard'))
- image_weight_grad: float32 [768, 1024], P(('dp', 'shard'))
- cross_query_grad: float32 [1024, 1024], P(('dp', 'shard'))
- cross_keyval_grad: float32 [1024, 2048], P(('dp', 'shard'))
- cross_output_grad: float32 [1024, 1024], P(('dp', 'shard'))
- second_gain_grad: float32 [1024], P(('dp', 'shard'))
- second_shift_grad: float32 [1024], P(('dp', 'shard'))
- self_project_grad: float32 [1024, 3072], P(('dp', 'shard'))
- self_output_grad: float32 [1024, 1024], P(('dp', 'shard'))
- third_gain_grad: float32 [1024], P(('dp', 'shard'))
- third_shift_grad: float32 [1024], P(('dp', 'shard'))
- hidden_weight_grad: float32 [1024, 4096], P(('dp', 'shard'))
- hidden_bias_grad: float32 [4096], P(('dp', 'shard'))
- output_weight_grad: float32 [4096, 1024], P(('dp', 'shard'))
- deconv_weight_grad: float32 [1024, 320], P(('dp', 'shard'))
The draws below stay inside these ranges and needn't reach their ends.
All inputs are finite; a program needn't handle non-finite values. No bound on the sum of `ray_mask` on one device may be relied on, other than what follows from the above.
Results may differ from the reference program's by a relative error of at most 0.019.
The reference program's roundings to bfloat16 on the way count: a program that leaves them out, or rounds other values in their place, can miss the bound.
Values may be sent and summed in bfloat16 or wider, within the bound.
No kernel may reach another device: no remote copies, remote signals or barrier semaphores. Data moves between devices by JAX's collectives and lax.ppermute only.
A program may use at most 320 MiB of HBM per device.

```python
import jax
import jax.numpy as jnp
from jax import lax

D = 1024
H = 16
HD = 64
FF = 4096
DINO = 768
CH = 80
G = 32
PATCH = 4096
RB = 128
SAMP = 32
OBJ_GRP = 2
NBLK = 2
OBJECTS = 8
TOK_OBJ = 3072
BLOCKS = 64
RAYS = 8192
POINTS = 262144
N_DP = 4
N_SHARD = 8


def draw_block_object(key, part):
    key = jax.random.fold_in(key, 11)
    per_group = NBLK * N_SHARD
    keys = jax.random.split(key, 3)
    heavy = jax.random.randint(keys[0], (N_DP, 1), 0, OBJ_GRP)
    coin = jax.random.randint(keys[1], (N_DP, per_group), 0, 8)
    other = jax.random.randint(keys[2], (N_DP, per_group), 0, OBJ_GRP)
    chosen = jnp.where(coin < 5, heavy, other)
    position = jnp.arange(per_group, dtype=jnp.int32)[None, :]
    chosen = jnp.where((position >= 1) & (position <= OBJ_GRP), position - 1, chosen)
    chosen = jnp.where((position == 0) | (position == per_group - 1), heavy, chosen)
    return chosen.reshape(N_DP * per_group).astype(jnp.int32)


def draw_sample_cell(key, part):
    key = jax.random.fold_in(key, 23)
    first, second = jax.random.split(key)
    side = 2 * G
    rows = jax.random.randint(first, (3, POINTS), 0, side - 1)
    cols = jax.random.randint(second, (3, POINTS), 0, side - 1)
    return (rows * side + cols).astype(jnp.int32)


def with_ends(entries, rng, least, high):
    spot = [jax.random.randint(jax.random.fold_in(rng, axis), (), 0, length) for axis, length in enumerate(entries.shape)]
    main_axis = entries.shape.index(max(entries.shape))
    next_to = spot[:main_axis] + [(spot[main_axis] + 1) % entries.shape[main_axis]] + spot[main_axis + 1:]
    return entries.at[tuple(spot)].set(least).at[tuple(next_to)].set(high)


def with_spikes(values, rng, source, target, blocks, factor):
    owner, partner = [(jnp.arange(values.shape[dim]) // (values.shape[dim] // blocks)).reshape([-1 if axis == dim else 1 for axis in range(values.ndim)]) for dim in (source, target)]
    chosen = jax.random.permutation(rng, blocks)[partner]
    strong = (owner == chosen) | (owner == (partner + blocks // 2) % blocks)
    return jnp.where(strong, factor * values, values)


def block_levels(stream_key, shape, shards, low, high):
    level, own = 1.0, jax.random.fold_in(stream_key, 6)
    for axis_at, blocks in shards:
        steps = jnp.exp(jax.random.uniform(jax.random.fold_in(own, axis_at), (blocks,), jnp.float32, low / len(shards), high / len(shards)))
        level = level * jnp.repeat(steps, shape[axis_at] // blocks).reshape([-1 if axis == axis_at else 1 for axis in range(len(shape))])
    return level


def noise(own_key, dims, width, limit, cuts=(), kind=jnp.bfloat16):
    values = jax.random.normal(own_key, dims, jnp.float32) * width
    if len(cuts) > 0:
        values = block_levels(own_key, dims, cuts, -0.22, 0.18) * values
    return jnp.clip(values, min=-limit, max=limit).astype(kind)


def gaussian_with(own_key, dims, deviation, bound, pieces, heavy, kind=jnp.bfloat16):
    array = deviation * jax.random.normal(own_key, dims, jnp.float32)
    if pieces:
        array = array * block_levels(own_key, dims, pieces, -0.22, 0.18)
    return jnp.clip(with_spikes(array, jax.random.fold_in(own_key, 3), *heavy), -bound, bound).astype(kind)


def setup_inputs(seed: int = 0) -> dict:
    streams_of = jax.random.split(jax.random.key(seed), 25)
    return {
        "tokens": noise(streams_of[0], (TOK_OBJ, OBJECTS, D), 1.0, 6.0, ((0, 8), (1, 4))),
        "dino": noise(streams_of[1], (PATCH, OBJECTS, DINO), 1.0, 6.0, ((0, 8), (1, 4))),
        "first_gain": jnp.clip(1.0 + 0.18 * jax.random.normal(streams_of[2], (D,), jnp.float32), 0.1, 1.9),
        "first_shift": noise(streams_of[3], (D,), 0.1, 0.625, ((0, 32),), jnp.float32),
        "image_weight": noise(streams_of[4], (DINO, D), DINO ** -0.5, 0.21875, ((0, 32),), jnp.float32),
        "cross_query": noise(streams_of[5], (D, D), D ** -0.5, 0.1875, ((0, 32),), jnp.float32),
        "cross_keyval": noise(streams_of[6], (D, 2 * D), D ** -0.5, 0.1875, ((0, 32),), jnp.float32),
        "cross_output": noise(streams_of[7], (D, D), (max(1, 3 * D // PATCH)) ** -0.5, 6.0, ((0, 32),), jnp.float32),
        "second_gain": jnp.clip(1.0 + 0.18 * jax.random.normal(streams_of[8], (D,), jnp.float32), 0.1, 1.9),
        "second_shift": noise(streams_of[9], (D,), 0.02, 0.125, ((0, 32),), jnp.float32),
        "self_project": noise(streams_of[10], (D, 3 * D), D ** -0.5, 0.1875, ((0, 32),), jnp.float32),
        "self_output": noise(streams_of[11], (D, D), (max(1, 3 * D // TOK_OBJ)) ** -0.5, 6.0, ((0, 32),), jnp.float32),
        "third_gain": jnp.clip(1.0 + 0.18 * jax.random.normal(streams_of[12], (D,), jnp.float32), 0.1, 1.9),
        "third_shift": noise(streams_of[13], (D,), 0.1, 0.625, ((0, 32),), jnp.float32),
        "hidden_weight": noise(streams_of[14], (D, FF), D ** -0.5, 0.1875, ((0, 32),), jnp.float32),
        "hidden_bias": noise(streams_of[15], (FF,), 0.3, 1.75, ((0, 32),), jnp.float32),
        "output_weight": noise(streams_of[16], (FF, D), FF ** -0.5, 0.09375, ((0, 32),), jnp.float32),
        "deconv_weight": noise(streams_of[17], (D, 4 * CH), D ** -0.5, 0.1875, ((0, 32),), jnp.float32),
        "ray_mask": with_ends((jax.random.randint(streams_of[18], (RAYS,), 0, 4) < 3).astype(jnp.int32), jax.random.fold_in(streams_of[18], 1), 0, 1),
        "block_object": draw_block_object(jax.random.fold_in(streams_of[24], 71), 0),
        "sample_cell": draw_sample_cell(jax.random.fold_in(streams_of[24], 71), 0),
        "sample_frac": jnp.clip(1.0 * jax.random.uniform(streams_of[21], (6, POINTS), jnp.float32) ** block_levels(streams_of[21], (6, POINTS), ((1, 32),), -0.2, 0.2), 0.0, 1.0),
        "out_grad": gaussian_with(streams_of[22], (TOK_OBJ, OBJECTS, D), 1.0, 8.0, ((0, 8), (1, 4)), (0, 2, 8, 2.0)),
        "sampled_grad": noise(streams_of[23], (RAYS, SAMP * CH), 1.0, 6.0, ((0, 32),)),
    }


@jax.custom_vjp
def low(v):
    return lax.optimization_barrier(v.astype(jnp.bfloat16)).astype(jnp.float32)

@jax.custom_vjp
def low_back(v):
    return v

def low_keep(v):
    return (low(v), None)

def low_pass(kept, grad):
    return (grad,)

def back_keep(v):
    return (v, None)

def back_low(kept, grad):
    return (low(grad),)
low.defvjp(low_keep, low_pass)
low_back.defvjp(back_keep, back_low)
highest = lax.Precision.HIGHEST
epsilon = 1e-05

def matmul(left, right):
    return jnp.dot(left, right, precision=highest, preferred_element_type=jnp.float32)

def rounded_both(value):
    return low(low_back(value))

def normalize(values, gain, shift):
    centered = values - lax.optimization_barrier(jnp.mean(values, axis=-1, keepdims=True))
    inverse = lax.rsqrt(lax.optimization_barrier(jnp.mean(centered * centered, axis=-1, keepdims=True)) + epsilon)
    return centered * inverse * gain + shift

def gelu(values):
    return 0.5 * values * (1.0 + lax.erf(values * 0.7071067811865476))

def attend_pair(parts):
    query, keys, values = parts
    scores = low_back(matmul(query, keys.T) * HD ** (-0.5))
    peak = lax.optimization_barrier(jnp.max(scores, axis=-1, keepdims=True))
    expo = jnp.exp(scores - peak)
    probability = expo / lax.optimization_barrier(jnp.sum(expo, axis=-1, keepdims=True))
    return matmul(low(probability), values)

def attention(query, keys, values):
    parts = (jnp.moveaxis(query, 1, 0), jnp.moveaxis(keys, 1, 0), jnp.moveaxis(values, 1, 0))
    return jnp.moveaxis(lax.map(jax.checkpoint(attend_pair), parts), 0, 1)

def sample_planes(planes, ray_mask, block_object, sample_cell, sample_frac):
    objects = planes.shape[1]
    table = jnp.moveaxis(planes, 1, 0).reshape(objects, TOK_OBJ * 4, CH)
    side = 2 * G
    ray_index = jnp.arange(RAYS * SAMP, dtype=jnp.int32) // SAMP
    block_index = ray_index // RB
    owner = block_index // (BLOCKS // N_DP) * OBJ_GRP + block_object[block_index]
    total = jnp.zeros((RAYS * SAMP, CH), planes.dtype)
    for plane in range(3):
        row_start = sample_cell[plane] // side
        col_start = sample_cell[plane] % side
        across = sample_frac[2 * plane]
        downward = sample_frac[2 * plane + 1]
        for drow in range(2):
            for dcol in range(2):
                pixel_row = row_start + drow
                pixel_col = col_start + dcol
                token = plane * G * G + pixel_row // 2 * G + pixel_col // 2
                flat = (token * 4 + pixel_row % 2 * 2 + pixel_col % 2).astype(jnp.int32)
                vertical = downward if drow == 1 else 1.0 - downward
                horizontal = across if dcol == 1 else 1.0 - across
                weight = low(vertical * horizontal)
                total = total + weight[:, None] * table[owner, flat]
    return total.reshape(RAYS, SAMP * CH) * ray_mask.astype(planes.dtype)[:, None]

def forward(floats, ray_mask, block_object, sample_cell, sample_frac):
    tokens, dino, first_gain, first_shift, image_weight, cross_query, cross_keyval, cross_output, second_gain, second_shift, self_project, self_output, third_gain, third_shift, hidden_weight, hidden_bias, output_weight, deconv_weight = floats
    objects = tokens.shape[1]
    pairs = objects * H
    normed = low(normalize(tokens, low(first_gain), low(first_shift)))
    query = rounded_both(matmul(normed, low(cross_query))).reshape(TOK_OBJ, pairs, HD)
    image = rounded_both(matmul(dino, low(image_weight)))
    keyval = rounded_both(matmul(image, low(cross_keyval))).reshape(PATCH, pairs, 2 * HD)
    mixed = rounded_both(attention(query, keyval[:, :, :HD], keyval[:, :, HD:])).reshape(TOK_OBJ, objects, D)
    after_cross = tokens + low_back(matmul(mixed, low(cross_output)))
    normed = low(normalize(after_cross, low(second_gain), low(second_shift)))
    projected = rounded_both(matmul(normed, low(self_project))).reshape(TOK_OBJ, pairs, 3 * HD)
    mixed = rounded_both(attention(projected[:, :, :HD], projected[:, :, HD:2 * HD], projected[:, :, 2 * HD:])).reshape(TOK_OBJ, objects, D)
    after_self = after_cross + low_back(matmul(mixed, low(self_output)))
    normed = low(normalize(after_self, low(third_gain), low(third_shift)))
    hidden = low_back(matmul(normed, low(hidden_weight)) + low(hidden_bias))
    result = after_self + low_back(matmul(low(gelu(hidden)), low(output_weight)))
    planes = rounded_both(matmul(low(result), low(deconv_weight)))
    sampled = sample_planes(planes, ray_mask, block_object, sample_cell, sample_frac)
    return (result, sampled)

def reference(tokens, dino, first_gain, first_shift, image_weight, cross_query, cross_keyval, cross_output, second_gain, second_shift, self_project, self_output, third_gain, third_shift, hidden_weight, hidden_bias, output_weight, deconv_weight, ray_mask, block_object, sample_cell, sample_frac, out_grad, sampled_grad):
    floats = (tokens.astype(jnp.float32), dino.astype(jnp.float32), first_gain, first_shift, image_weight, cross_query, cross_keyval, cross_output, second_gain, second_shift, self_project, self_output, third_gain, third_shift, hidden_weight, hidden_bias, output_weight, deconv_weight)
    fractions = sample_frac.astype(jnp.float32)

    def closed(values):
        return forward(values, ray_mask, block_object, sample_cell, fractions)
    (result, sampled), pullback = jax.vjp(closed, floats)
    grads = pullback((out_grad.astype(jnp.float32), sampled_grad.astype(jnp.float32)))[0]
    return (result.astype(jnp.bfloat16), sampled.astype(jnp.bfloat16), grads[0], grads[1], grads[2], grads[3], grads[4], grads[5], grads[6], grads[7], grads[8], grads[9], grads[10], grads[11], grads[12], grads[13], grads[14], grads[15], grads[16], grads[17])
```

```python
import functools
import math

import jax
import jax.numpy as jnp
from jax import lax
from jax.experimental import pallas as pl
from jax.experimental.pallas import tpu as pltpu
from jax.sharding import Mesh
from jax.sharding import PartitionSpec as P

D = 1024
H = 16
HD = 64
FF = 4096
DINO = 768
CH = 80
G = 32
RB = 128
SAMP = 32
TOK_OBJ = 3072
PIX = G * G
SCALE = HD ** (-0.5)
VMEM = 58 * 2**20

epsilon = 1e-05
NN = ((1,), (0,))
NT = ((1,), (1,))
TN = ((0,), (0,))
bf16 = jnp.bfloat16
f32 = jnp.float32


def lower(value):
    return value.astype(bf16)


def widen(value):
    return value.astype(f32)


def dot(left, right, dims):
    return lax.dot_general(left, right, (dims, ((), ())), preferred_element_type=f32)


def normalize(values, gain, shift):
    centered = values - jnp.mean(values, axis=-1, keepdims=True)
    inverse = lax.rsqrt(jnp.mean(centered * centered, axis=-1, keepdims=True) + epsilon)
    unit = centered * inverse
    return (unit * gain + shift, unit, inverse)


def normalize_back(grad, unit, inverse, gain):
    gain_grad = jnp.sum(grad * unit, axis=0)
    shift_grad = jnp.sum(grad, axis=0)
    scaled = grad * gain
    inner = (
        scaled
        - jnp.mean(scaled, axis=-1, keepdims=True)
        - unit * jnp.mean(scaled * unit, axis=-1, keepdims=True)
    )
    return (inverse * inner, gain_grad, shift_grad)


def gelu(values):
    return 0.5 * values * (1.0 + lax.erf(values * 0.7071067811865476))


def fixed(shape):
    return pl.BlockSpec(shape, lambda *_: (0,) * len(shape))


def forward_kernel(*refs, chunks, block, packed):
    q_refs, refs = refs[:chunks], refs[chunks:]
    if packed:
        kv_refs = q_refs
    else:
        kv_refs, refs = refs[:chunks], refs[chunks:]
    out_refs, refs = refs[:chunks], refs[chunks:]
    lse_ref, query_ref, keys_ref = refs
    first = HD if packed else 0
    turn = pl.program_id(0)

    @pl.when(turn == 0)
    def _():
        for r in range(chunks):
            keys_ref[r] = kv_refs[r][first : first + HD, :].T
            query_ref[r] = q_refs[r][:HD, :] * jnp.asarray(SCALE, bf16)

    query = query_ref[turn]
    count = query.shape[1]
    peak = jnp.full((1, count), -jnp.inf, f32)
    total = jnp.zeros((1, count), f32)
    mixed = jnp.zeros((HD, count), f32)
    places = [(r, c) for r in range(chunks) for c in range(0, keys_ref.shape[1], block)]

    def score(place):
        r, c = place
        return dot(keys_ref[r, c : c + block, :], query, NN)

    ahead = score(places[0])
    for step, (r, c) in enumerate(places):
        scores = ahead
        if step + 1 < len(places):
            ahead = score(places[step + 1])
        higher = jnp.maximum(peak, jnp.max(scores, axis=0, keepdims=True))
        expo = jnp.exp(scores - higher)
        shrink = jnp.exp(peak - higher)
        total = total * shrink + jnp.sum(expo, axis=0, keepdims=True)
        values = kv_refs[r][first + HD : first + 2 * HD, c : c + block]
        mixed = mixed * shrink + dot(values, lower(expo), NN)
        peak = higher
    out = lower(mixed / total)
    for r in range(chunks):

        @pl.when(turn == r)
        def _():
            out_refs[r][...] = out

    lse_ref[0] = peak + jnp.log(total)


def attend_forward(queries, keyvals):
    packed = keyvals is None
    sources = list(queries) if packed else list(queries) + list(keyvals)
    chunks = len(queries)
    count = queries[0].shape[1]
    length = sources[-1].shape[1]
    block = math.gcd(length, 256)
    steps = chunks * chunks * count * length
    *outs, lse = pl.pallas_call(
        functools.partial(forward_kernel, chunks=chunks, block=block, packed=packed),
        grid=(chunks,),
        in_specs=[fixed(s.shape) for s in sources],
        out_specs=[fixed((HD, count))] * chunks + [pl.BlockSpec((1, 1, count), lambda i: (i, 0, 0))],
        out_shape=[jax.ShapeDtypeStruct((HD, count), bf16)] * chunks
        + [jax.ShapeDtypeStruct((chunks, 1, count), f32)],
        scratch_shapes=[
            pltpu.VMEM((chunks, HD, count), bf16),
            pltpu.VMEM((chunks, length, HD), bf16),
        ],
        compiler_params=pltpu.CompilerParams(vmem_limit_bytes=VMEM),
        cost_estimate=pl.CostEstimate(
            flops=steps * 2 * 2 * 256, bytes_accessed=4 * chunks * length * 64, transcendentals=steps
        ),
        name="attend_forward",
    )(*sources)
    return outs, lse


def backward_kernel(*refs, chunks, block, packed):
    q_refs, refs = refs[:chunks], refs[chunks:]
    if packed:
        kv_refs = q_refs
    else:
        kv_refs, refs = refs[:chunks], refs[chunks:]
    dout_refs, out_refs, refs = refs[:chunks], refs[chunks : 2 * chunks], refs[2 * chunks :]
    lse_ref, refs = refs[0], refs[1:]
    query_grads, refs = refs[:chunks], refs[chunks:]
    if packed:
        grads = query_grads
    else:
        grads, refs = refs[:chunks], refs[chunks:]
    query_ref, dout_ref, delta_ref, keys_ref, keys_acc, values_acc = refs
    first = HD if packed else 0
    turn = pl.program_id(0)
    length = keys_ref.shape[1]

    @pl.when(turn == 0)
    def _():
        for r in range(chunks):
            keys_ref[r] = kv_refs[r][first : first + HD, :].T
            query_ref[r] = q_refs[r][:HD, :] * jnp.asarray(SCALE, bf16)
            dout_ref[r] = dout_refs[r][...]
            delta_ref[r] = jnp.sum(
                widen(dout_refs[r][...]) * widen(out_refs[r][...]), axis=0, keepdims=True
            )
        keys_acc[...] = jnp.zeros_like(keys_acc)
        values_acc[...] = jnp.zeros_like(values_acc)

    query = query_ref[turn]
    dout = dout_ref[turn]
    count = query.shape[1]

    def across(row):
        if block % 128:
            return jnp.broadcast_to(row, (block, count)).T
        return jnp.concatenate([jnp.broadcast_to(row, (128, count)).T] * (block // 128), axis=1)

    lse_cols = across(lse_ref[0])
    delta_cols = across(delta_ref[turn])
    query_rows = query.T
    dout_rows = dout.T
    query_grad = jnp.zeros((count, HD), f32)
    places = [(r, c) for r in range(chunks) for c in range(0, length, block)]

    def score(place):
        r, c = place
        span = slice(c, c + block)
        return (
            dot(query_rows, kv_refs[r][first : first + HD, span], NN),
            dot(dout_rows, kv_refs[r][first + HD : first + 2 * HD, span], NN),
        )

    ahead = score(places[0])
    for step, (r, c) in enumerate(places):
        scores, prob_grad = ahead
        if step + 1 < len(places):
            ahead = score(places[step + 1])
        span = slice(c, c + block)
        probability = jnp.exp(scores - lse_cols)
        score_grad = lower(probability * (prob_grad - delta_cols))
        query_grad = query_grad + dot(score_grad, keys_ref[r, span, :], NN)
        values_acc[r, :, span] += dot(dout, lower(probability), NN)
        keys_acc[r, :, span] += dot(query, score_grad, NN)
    query_grad = lower((query_grad * SCALE).T)
    for r in range(chunks):

        @pl.when(turn == r)
        def _():
            query_grads[r][:HD, :] = query_grad

    @pl.when(turn == chunks - 1)
    def _():
        for r in range(chunks):
            grads[r][first : first + HD, :] = lower(keys_acc[r])
            grads[r][first + HD : first + 2 * HD, :] = lower(values_acc[r])


def attend_backward(queries, keyvals, douts, outs, lse):
    packed = keyvals is None
    sources = list(queries) if packed else list(queries) + list(keyvals)
    chunks = len(queries)
    count = queries[0].shape[1]
    length = sources[-1].shape[1]
    block = math.gcd(length, 256)
    steps = chunks * chunks * count * length
    results = [s.shape for s in sources]
    sources = sources + list(douts) + list(outs)
    grads = pl.pallas_call(
        functools.partial(backward_kernel, chunks=chunks, block=block, packed=packed),
        grid=(chunks,),
        in_specs=[fixed(s.shape) for s in sources] + [pl.BlockSpec((1, 1, count), lambda i: (i, 0, 0))],
        out_specs=[fixed(s) for s in results],
        out_shape=[jax.ShapeDtypeStruct(s, bf16) for s in results],
        scratch_shapes=[
            pltpu.VMEM((chunks, HD, count), bf16),
            pltpu.VMEM((chunks, HD, count), bf16),
            pltpu.VMEM((chunks, 1, count), f32),
            pltpu.VMEM((chunks, length, HD), bf16),
            pltpu.VMEM((chunks, HD, length), f32),
            pltpu.VMEM((chunks, HD, length), f32),
        ],
        compiler_params=pltpu.CompilerParams(vmem_limit_bytes=VMEM),
        cost_estimate=pl.CostEstimate(
            flops=steps * 2 * 5 * 200, bytes_accessed=8 * chunks * length * 64, transcendentals=steps
        ),
        name="attend_backward",
    )(*sources, lse)
    return grads[:chunks], grads[chunks:]


def split_kernel(me_ref, source_ref, *out_refs, heads):
    turn = pl.program_id(0)
    for k in range(len(out_refs) // heads):

        @pl.when(turn == k)
        def _():
            for j in range(heads):
                out_refs[k * heads + j][...] = source_ref[0, j]


def split(values, me):
    chunks, heads, height, count = values.shape
    outs = pl.pallas_call(
        functools.partial(split_kernel, heads=heads),
        grid_spec=pltpu.PrefetchScalarGridSpec(
            num_scalar_prefetch=1,
            grid=(chunks,),
            in_specs=[pl.BlockSpec((1, heads, height, count), lambda k, m: (m[0] ^ k, 0, 0, 0))],
            out_specs=[fixed((height, count))] * (chunks * heads),
        ),
        out_shape=[jax.ShapeDtypeStruct((height, count), bf16)] * (chunks * heads),
        compiler_params=pltpu.CompilerParams(vmem_limit_bytes=VMEM),
        cost_estimate=pl.CostEstimate(flops=0, bytes_accessed=4 * values.size, transcendentals=0),
        name="split",
    )(me, values)
    return [[outs[k * heads + j] for k in range(chunks)] for j in range(heads)]


def assemble_kernel(me_ref, *refs, heads):
    turn = pl.program_id(0)
    out_ref = refs[-1]
    for k in range((len(refs) - 1) // heads):

        @pl.when(turn == k)
        def _():
            for j in range(heads):
                out_ref[0, j] = refs[k * heads + j][...]


def assemble(parts, me):
    heads, chunks = len(parts), len(parts[0])
    height, count = parts[0][0].shape
    sources = [parts[j][k] for k in range(chunks) for j in range(heads)]
    return pl.pallas_call(
        functools.partial(assemble_kernel, heads=heads),
        grid_spec=pltpu.PrefetchScalarGridSpec(
            num_scalar_prefetch=1,
            grid=(chunks,),
            in_specs=[fixed((height, count))] * (chunks * heads),
            out_specs=pl.BlockSpec((1, heads, height, count), lambda k, m: (m[0] ^ k, 0, 0, 0)),
        ),
        out_shape=jax.ShapeDtypeStruct((chunks, heads, height, count), bf16),
        compiler_params=pltpu.CompilerParams(vmem_limit_bytes=VMEM),
        cost_estimate=pl.CostEstimate(
            flops=0, bytes_accessed=4 * chunks * heads * height * count, transcendentals=0
        ),
        name="assemble",
    )(me, *sources)


def tap_rows(cell_ref, frac_ref, live, plane, points):
    cell = cell_ref[0, plane : plane + 1, points]
    row = cell // (2 * G)
    col = cell - row * (2 * G)
    across = frac_ref[0, 2 * plane : 2 * plane + 1, points]
    downward = frac_ref[0, 2 * plane + 1 : 2 * plane + 2, points]
    half = lax.broadcasted_iota(jnp.int32, (G, cell.shape[1]), 0) * 2

    def spread(start, fraction, odd, gate):
        place = half + odd
        return jnp.where(
            place == start,
            (1.0 - fraction) * gate,
            jnp.where(place == start + 1, fraction * gate, 0.0),
        )

    return (
        [spread(row, downward, odd, live) for odd in range(2)],
        [spread(col, across, odd, 1.0) for odd in range(2)],
    )


def tap_table(table_ref, down, side):
    for ty in range(G):
        table_ref[ty * G : (ty + 1) * G, :] = lower(down[ty : ty + 1, :] * side)


def sample_kernel(object_ref, cell_ref, frac_ref, live_ref, plane_ref, out_ref, table_ref, picked_ref, *, width):
    turn = pl.program_id(1)
    lanes = pl.ds(pl.multiple_of(turn * width, width), width)
    live = jnp.concatenate([live_ref[0]] * (width // RB), axis=1)
    picked = jnp.zeros((CH, width), f32)
    slot = 0
    for plane in range(3):
        downs, sides = tap_rows(cell_ref, frac_ref, live, plane, lanes)
        for dy in range(2):
            for dx in range(2):
                tap_table(table_ref.at[slot], downs[dy], sides[dx])
                part = (2 * dy + dx) * CH
                features = plane_ref[0, part : part + CH, plane * PIX : (plane + 1) * PIX]
                picked = picked + dot(features, table_ref[slot], NN)
                slot = 1 - slot
    picked_ref[:, lanes] = picked

    @pl.when(turn == pl.num_programs(1) - 1)
    def _():
        for s in range(SAMP):
            out_ref[:, s * CH : (s + 1) * CH] = lower(picked_ref[:, s * RB : (s + 1) * RB].T)


def sample_points(planes, owners, cells, fractions, live):
    blocks = owners.shape[0]
    points = RB * SAMP
    width = 512
    return pl.pallas_call(
        functools.partial(sample_kernel, width=width),
        grid_spec=pltpu.PrefetchScalarGridSpec(
            num_scalar_prefetch=1,
            grid=(blocks, points // width),
            in_specs=[
                pl.BlockSpec((1, 3, points), lambda b, t, o: (b, 0, 0)),
                pl.BlockSpec((1, 6, points), lambda b, t, o: (b, 0, 0)),
                pl.BlockSpec((1, 1, RB), lambda b, t, o: (b, 0, 0)),
                pl.BlockSpec((1, 4 * CH, TOK_OBJ), lambda b, t, o: (o[b], 0, 0)),
            ],
            out_specs=pl.BlockSpec((RB, SAMP * CH), lambda b, t, o: (b, 0)),
            scratch_shapes=[
                pltpu.VMEM((2, PIX, width), bf16),
                pltpu.VMEM((CH, points), f32),
            ],
        ),
        out_shape=jax.ShapeDtypeStruct((blocks * RB, SAMP * CH), bf16),
        compiler_params=pltpu.CompilerParams(vmem_limit_bytes=VMEM),
        cost_estimate=pl.CostEstimate(
            flops=blocks * points * 3 * 4096 * 2 * 256,
            bytes_accessed=blocks * 5 * 2**20,
            transcendentals=0,
        ),
        name="sample_points",
    )(owners, cells, fractions, live, planes)


def scatter_kernel(object_ref, cell_ref, frac_ref, live_ref, grad_ref, out_ref, table_ref, rows_ref, total_ref, *, width):
    block = pl.program_id(0)
    turn = pl.program_id(1)
    owner = object_ref[block]

    @pl.when((block == 0) & (turn == 0))
    def _():
        total_ref[...] = jnp.zeros_like(total_ref)

    @pl.when(turn == 0)
    def _():
        for s in range(SAMP):
            rows_ref[:, s * RB : (s + 1) * RB] = grad_ref[:, s * CH : (s + 1) * CH].T

    lanes = pl.ds(pl.multiple_of(turn * width, width), width)
    live = jnp.concatenate([live_ref[0]] * (width // RB), axis=1)
    grads = rows_ref[:, lanes]
    slot = 0
    for plane in range(3):
        downs, sides = tap_rows(cell_ref, frac_ref, live, plane, lanes)
        for dy in range(2):
            for dx in range(2):
                tap_table(table_ref.at[slot], downs[dy], sides[dx])
                part = (2 * dy + dx) * CH
                total_ref[owner, part : part + CH, plane * PIX : (plane + 1) * PIX] += dot(
                    grads, table_ref[slot], NT
                )
                slot = 1 - slot

    @pl.when((block == pl.num_programs(0) - 1) & (turn == pl.num_programs(1) - 1))
    def _():
        out_ref[...] = lower(total_ref[...])


def scatter_points(grads, owners, cells, fractions, live, objects):
    blocks = owners.shape[0]
    points = RB * SAMP
    width = 512
    shape = (objects, 4 * CH, TOK_OBJ)
    return pl.pallas_call(
        functools.partial(scatter_kernel, width=width),
        grid_spec=pltpu.PrefetchScalarGridSpec(
            num_scalar_prefetch=1,
            grid=(blocks, points // width),
            in_specs=[
                pl.BlockSpec((1, 3, points), lambda b, t, o: (b, 0, 0)),
                pl.BlockSpec((1, 6, points), lambda b, t, o: (b, 0, 0)),
                pl.BlockSpec((1, 1, RB), lambda b, t, o: (b, 0, 0)),
                pl.BlockSpec((RB, SAMP * CH), lambda b, t, o: (b, 0)),
            ],
            out_specs=pl.BlockSpec(shape, lambda b, t, o: (0, 0, 0)),
            scratch_shapes=[
                pltpu.VMEM((2, PIX, width), bf16),
                pltpu.VMEM((CH, points), bf16),
                pltpu.VMEM(shape, f32),
            ],
        ),
        out_shape=jax.ShapeDtypeStruct(shape, bf16),
        compiler_params=pltpu.CompilerParams(vmem_limit_bytes=VMEM),
        cost_estimate=pl.CostEstimate(
            flops=blocks * points * 3 * 4096 * 2 * 256,
            bytes_accessed=blocks * 5 * 2**20,
            transcendentals=0,
        ),
        name="scatter_points",
    )(owners, cells, fractions, live, grads)


SWAP = [(0, 1), (1, 0)]


def body(
    dp_axes,
    group_axes,
    tokens,
    dino,
    first_gain,
    first_shift,
    image_weight,
    cross_query,
    cross_keyval,
    cross_output,
    second_gain,
    second_shift,
    self_project,
    self_output,
    third_gain,
    third_shift,
    hidden_weight,
    hidden_bias,
    output_weight,
    deconv_weight,
    ray_mask,
    block_object,
    sample_cell,
    sample_frac,
    out_grad,
    sampled_grad,
):
    shard_axes = ("h",) + group_axes
    every = dp_axes + shard_axes
    outer, core = dp_axes
    group = 2 ** len(group_axes)
    heads = H // group
    half = lax.axis_index("h")
    side = lax.axis_index(core)
    over = lax.axis_index(outer)
    place = lax.axis_index(group_axes)
    me = place.reshape(1).astype(jnp.int32)
    rows = tokens.shape[0]
    count = 2 * rows
    patches = 2 * dino.shape[0]
    share = first_gain.shape[0]
    join = lax.optimization_barrier

    def own_object(values):
        mine = lax.dynamic_index_in_dim(values, half, 1, keepdims=False)
        other = lax.dynamic_index_in_dim(values, 1 - half, 1, keepdims=False)
        got = lax.ppermute(other, "h", SWAP)
        return jnp.concatenate(
            [jnp.where(half == 0, mine, got), jnp.where(half == 0, got, mine)], axis=0
        )

    def both_objects(values):
        size = values.shape[0] // 2
        mine = lax.dynamic_slice_in_dim(values, half * size, size, 0)
        away = lower(lax.dynamic_slice_in_dim(values, (1 - half) * size, size, 0))
        got = lax.ppermute(away, "h", SWAP).astype(mine.dtype)
        return jnp.stack(
            [jnp.where(half == 0, mine, got), jnp.where(half == 0, got, mine)], axis=1
        )

    def gather(pieces):
        return lax.all_gather(jnp.concatenate(pieces, axis=1), every, axis=0, tiled=True)

    def exchange(chunks):
        return [chunks[0]] + [
            lax.ppermute(chunks[k], group_axes, [(i, i ^ k) for i in range(group)])
            for k in range(1, group)
        ]

    def exchange_all(parts):
        done = []
        for chunks in parts:
            if done:
                chunks, done[-1] = join((chunks, done[-1]))
            done.append(exchange(chunks))
        return done

    columns = jnp.stack(
        [first_gain, first_shift, second_gain, second_shift, third_gain, third_shift], axis=1
    )
    columns = jnp.concatenate([columns, hidden_bias.reshape(share, FF // D)], axis=1)
    columns = jnp.pad(columns, ((0, 0), (0, 128 - columns.shape[1])))
    early = gather(
        [
            lower(cross_query),
            lower(cross_keyval),
            lower(image_weight).reshape(share, DINO),
            lower(columns),
        ]
    )
    middle = gather([lower(cross_output), lower(self_project), lower(self_output)])
    late = gather([lower(hidden_weight), lower(deconv_weight)])
    output_w = lax.all_gather(lower(output_weight), every, axis=0, tiled=True)
    query_w = early[:, :D]
    keyval_w = early[:, D : 3 * D]
    image_w = early[:, 3 * D : 3 * D + DINO].reshape(DINO, D)
    vectors = widen(early[:, 3 * D + DINO :])
    gain_a, shift_a, gain_b, shift_b, gain_c, shift_c = [vectors[:, i] for i in range(6)]
    bias = vectors[:, 6 : 6 + FF // D].reshape(FF)
    cross_w = middle[:, :D]
    project_w = middle[:, D : 4 * D]
    self_w = middle[:, 4 * D :]
    hidden_w = late[:, :FF]
    deconv_w = late[:, FF:]

    blocks = ray_mask.shape[0] // RB

    def by_sample(values):
        kinds = values.shape[0]
        values = values.reshape(kinds, blocks, RB, SAMP)
        return values.transpose(1, 0, 3, 2).reshape(blocks, kinds, SAMP * RB)

    cells = by_sample(sample_cell)
    fractions = by_sample(sample_frac)
    live = widen(ray_mask).reshape(blocks, 1, RB)
    plane_grad = scatter_points(sampled_grad, block_object, cells, fractions, live, 2)
    token_low = own_object(tokens)
    dino_values = own_object(dino)
    plane_grad, token_low, dino_values = join((plane_grad, token_low, dino_values))
    out_cotangent = own_object(out_grad)
    parts = plane_grad.reshape(2, 4 * CH, 2, group, rows)
    parts = parts.transpose(0, 3, 1, 2, 4).reshape(2 * group * 4 * CH, count)
    plane_low = lax.psum_scatter(parts, shard_axes, scatter_dimension=0, tiled=True)
    token_values = widen(token_low)

    normed_full, unit_a, inverse_a = normalize(token_values, gain_a, shift_a)
    normed_a = lower(normed_full)
    image = lower(dot(dino_values, image_w, NN))
    queries = lower(dot(query_w, normed_a, ((0,), (1,)))).reshape(group, heads, HD, count)
    keyvals = lower(dot(keyval_w, image, ((0,), (1,)))).reshape(group, heads, 2 * HD, patches)
    queries, keyvals = split(queries, me), split(keyvals, me)
    sent = exchange_all([list(zip(queries[j], keyvals[j])) for j in range(heads)])
    cross_q = [[c[0] for c in x] for x in sent]
    cross_kv = [[c[1] for c in x] for x in sent]
    cross_out = [attend_forward(q, kv) for q, kv in zip(cross_q, cross_kv)]
    cross_mix = assemble([exchange(o) for o, _ in cross_out], me).reshape(D, count)
    after_cross = token_values + dot(cross_mix, cross_w, TN)

    normed_full, unit_b, inverse_b = normalize(after_cross, gain_b, shift_b)
    normed_b = lower(normed_full)
    projected = lower(dot(project_w, normed_b, ((0,), (1,)))).reshape(group, heads, 3 * HD, count)
    self_qkv = exchange_all(split(projected, me))
    self_out = [attend_forward(x, None) for x in self_qkv]
    self_mix = assemble([exchange(o) for o, _ in self_out], me).reshape(D, count)
    after_self = after_cross + dot(self_mix, self_w, TN)

    normed_full, unit_c, inverse_c = normalize(after_self, gain_c, shift_c)
    normed_c = lower(normed_full)
    hidden = dot(normed_c, hidden_w, NN) + bias
    activated = lower(gelu(hidden))
    result_low = lower(after_self + dot(activated, output_w, NN))
    tokens_out = both_objects(result_low)

    planes = lower(dot(deconv_w, result_low, ((0,), (1,))))
    plane_all = lax.all_gather(planes, shard_axes, axis=0, tiled=True)
    plane_all = plane_all.reshape(2, group, 4 * CH, 2, rows).transpose(0, 2, 3, 1, 4)
    plane_all = plane_all.reshape(2, 4 * CH, TOK_OBJ)

    def dp_grad(left, axis, right, right_axis):
        quarter = left.shape[axis] // 4
        dims = ((1 - axis,), (right_axis,))

        def block(y, c):
            part = lax.dynamic_slice_in_dim(left, (2 * y + c) * quarter, quarter, axis)
            return dot(part, right, dims)

        def chip(y):
            away = lower(block(y, 1 - side))
            return block(y, side) + widen(lax.ppermute(away, core, SWAP))

        other = lower(chip(1 - over))
        return lower(chip(over) + widen(lax.ppermute(other, outer, SWAP)))

    def scatter_sum(values):
        return widen(lax.psum_scatter(values, shard_axes, scatter_dimension=0, tiled=True))

    result_grad = widen(out_cotangent) + dot(plane_low, deconv_w, ((0,), (1,)))
    result_low_grad = lower(result_grad)
    activated_grad = dot(result_low_grad, output_w, NT)
    _, gelu_pull = jax.vjp(gelu, hidden)
    hidden_grad = lower(gelu_pull(activated_grad)[0])
    bias_grad = jnp.sum(widen(hidden_grad), axis=0)
    output_part = dp_grad(activated, 1, result_low_grad, 0)
    hidden_part = dp_grad(normed_c, 1, hidden_grad, 0)
    back_c, gain_c_grad, shift_c_grad = normalize_back(
        dot(hidden_grad, hidden_w, NT), unit_c, inverse_c, gain_c
    )
    self_grad = result_grad + back_c

    self_low = lower(self_grad)
    self_part = jnp.concatenate(
        [dp_grad(self_mix, 0, self_low, 0), dp_grad(result_low, 1, plane_low, 1)], axis=1
    )
    self_mix_grad = lower(dot(self_w, self_low, NT)).reshape(group, heads, HD, count)
    self_dout = exchange_all(split(self_mix_grad, me))
    self_dout[0], output_part, hidden_part, self_part = join(
        (self_dout[0], output_part, hidden_part, self_part)
    )
    output_weight_grad = scatter_sum(output_part)
    hidden_weight_grad = scatter_sum(hidden_part)
    self_sum = scatter_sum(self_part)
    self_back = [
        attend_backward(self_qkv[j], None, self_dout[j], *self_out[j])[0] for j in range(heads)
    ]
    project_grad = assemble([exchange(g) for g in self_back], me).reshape(3 * D, count)
    back_b, gain_b_grad, shift_b_grad = normalize_back(
        dot(project_grad, project_w, ((0,), (1,))), unit_b, inverse_b, gain_b
    )
    cross_grad = self_grad + back_b

    cross_low = lower(cross_grad)
    cross_mix_grad = lower(dot(cross_w, cross_low, NT)).reshape(group, heads, HD, count)
    cross_dout = exchange_all(split(cross_mix_grad, me))
    project_part = dp_grad(normed_b, 1, project_grad, 1)
    cross_part = dp_grad(cross_mix, 0, cross_low, 0)
    cross_dout[-1], project_part, cross_part = join((cross_dout[-1], project_part, cross_part))
    project_weight_grad = scatter_sum(project_part)
    cross_back = [
        attend_backward(cross_q[j], cross_kv[j], cross_dout[j], *cross_out[j])
        for j in range(heads)
    ]
    query_parts = [exchange(g) for g, _ in cross_back]
    keyval_parts = [exchange(g) for _, g in cross_back]
    query_back = assemble(query_parts, me).reshape(D, count)
    keyval_back = assemble(keyval_parts, me).reshape(2 * D, patches)
    image_grad = lower(dot(keyval_back, keyval_w, ((0,), (1,))))
    keyval_part = dp_grad(image, 1, keyval_back, 1)
    image_part = dp_grad(dino_values, 1, image_grad, 0)
    query_part = dp_grad(normed_a, 1, query_back, 1)
    back_a, gain_a_grad, shift_a_grad = normalize_back(
        dot(query_back, query_w, ((0,), (1,))), unit_a, inverse_a, gain_a
    )
    dino_grad = both_objects(dot(image_grad, image_w, NT))
    tokens_grad = both_objects(cross_grad + back_a)

    sums = jnp.stack(
        [gain_a_grad, shift_a_grad, gain_b_grad, shift_b_grad, gain_c_grad, shift_c_grad], axis=1
    )
    sums = jnp.concatenate([sums, bias_grad.reshape(D, FF // D)], axis=1)
    sums = jnp.pad(sums, ((0, 0), (0, 128 - sums.shape[1])))

    def quarter_rows(y, c):
        return lax.dynamic_slice_in_dim(sums, (2 * y + c) * (D // 4), D // 4, 0)

    def chip_rows(y):
        return quarter_rows(y, side) + lax.ppermute(quarter_rows(y, 1 - side), core, SWAP)

    vector_part = lower(chip_rows(over) + lax.ppermute(chip_rows(1 - over), outer, SWAP))
    last_part = jnp.concatenate([cross_part, keyval_part, query_part, vector_part], axis=1)
    last = scatter_sum(last_part)
    image_sum = scatter_sum(image_part)
    vector_sums = last[:, 4 * D :]

    late_cells, _ = join((cells, (keyval_part, image_part, query_part)))
    sampled = sample_points(plane_all, block_object, late_cells, fractions, live)

    return (
        tokens_out,
        sampled,
        tokens_grad,
        dino_grad,
        vector_sums[:, 0],
        vector_sums[:, 1],
        image_sum,
        last[:, 3 * D : 4 * D],
        last[:, D : 3 * D],
        last[:, :D],
        vector_sums[:, 2],
        vector_sums[:, 3],
        project_weight_grad,
        self_sum[:, :D],
        vector_sums[:, 4],
        vector_sums[:, 5],
        hidden_weight_grad,
        vector_sums[:, 6 : 6 + FF // D].reshape(share * (FF // D)),
        output_weight_grad,
        self_sum[:, D:],
    )


def solution(mesh):
    dp_bits = mesh.shape["dp"].bit_length() - 1
    shard_bits = mesh.shape["shard"].bit_length() - 1
    dp_axes = tuple(f"d{i}" for i in range(dp_bits))
    group_axes = tuple(f"r{i}" for i in range(shard_bits - 1))
    shard_axes = ("h",) + group_axes
    fine = Mesh(mesh.devices.reshape((2,) * (dp_bits + shard_bits)), dp_axes + shard_axes)
    every = dp_axes + shard_axes
    rows = P(shard_axes, dp_axes, None)
    vector = P(every)
    matrix = P(every, None)
    points = P(None, every)
    return jax.shard_map(
        functools.partial(body, dp_axes, group_axes),
        mesh=fine,
        in_specs=(
            rows, rows,
            vector, vector, matrix, matrix, matrix, matrix,
            vector, vector, matrix, matrix,
            vector, vector, matrix, vector, matrix, matrix,
            vector, vector, points, points, rows, matrix,
        ),
        out_specs=(
            rows, matrix, rows, rows,
            vector, vector, matrix, matrix, matrix, matrix,
            vector, vector, matrix, matrix,
            vector, vector, matrix, vector, matrix, matrix,
        ),
        check_vma=False,
    )
```

```python
import functools
import math

import jax
import jax.numpy as jnp
from jax import lax
from jax.experimental import pallas as pl
from jax.experimental.pallas import tpu as pltpu
from jax.sharding import Mesh
from jax.sharding import PartitionSpec as P

D = 1024
H = 16
HD = 64
FF = 4096
DINO = 768
CH = 80
G = 32
RB = 128
SAMP = 32
TOK_OBJ = 3072
PIX = G * G
SCALE = HD ** (-0.5)
VMEM = 58 * 2**20
ONES = 16

epsilon = 1e-05
NN = ((1,), (0,))
NT = ((1,), (1,))
TN = ((0,), (0,))
bf16 = jnp.bfloat16
f32 = jnp.float32


def lower(value):
    return value.astype(bf16)


def widen(value):
    return value.astype(f32)


def dot(left, right, dims):
    return lax.dot_general(left, right, (dims, ((), ())), preferred_element_type=f32)


def normalize(values, gain, shift):
    centered = values - jnp.mean(values, axis=-1, keepdims=True)
    inverse = lax.rsqrt(jnp.mean(centered * centered, axis=-1, keepdims=True) + epsilon)
    unit = centered * inverse
    return (unit * gain + shift, unit, inverse)


def normalize_back(grad, unit, inverse, gain):
    gain_grad = jnp.sum(grad * unit, axis=0)
    shift_grad = jnp.sum(grad, axis=0)
    scaled = grad * gain
    inner = (
        scaled
        - jnp.mean(scaled, axis=-1, keepdims=True)
        - unit * jnp.mean(scaled * unit, axis=-1, keepdims=True)
    )
    return (inverse * inner, gain_grad, shift_grad)


def gelu(values):
    return 0.5 * values * (1.0 + lax.erf(values * 0.7071067811865476))


def fixed(shape):
    return pl.BlockSpec(shape, lambda *_: (0,) * len(shape))


class Places:
    def __init__(self, shape, count):
        self.beside = shape[0] == HD
        self.count = count
        self.length = (shape[1] - count) // 2 if self.beside else shape[1]

    def query(self):
        return (slice(0, HD), slice(0, self.count))

    def keys(self, start, stop):
        if self.beside:
            return (slice(0, HD), slice(self.count + start, self.count + stop))
        return (slice(HD, 2 * HD), slice(start, stop))

    def values(self, start, stop):
        if self.beside:
            return self.keys(self.length + start, self.length + stop)
        return (slice(2 * HD, 3 * HD), slice(start, stop))


def forward_kernel(*refs, chunks, block, places):
    refs, out_refs = refs[:chunks], refs[chunks:]
    out_refs, (lse_ref, query_ref, keys_ref, values_ref) = out_refs[:chunks], out_refs[chunks:]
    turn = pl.program_id(0)
    length = places.length

    @pl.when(turn == 0)
    def _():
        for r in range(chunks):
            keys_ref[r] = refs[r][places.keys(0, length)].T
            query_ref[r] = refs[r][places.query()] * jnp.asarray(SCALE, bf16)
            values_ref[r, :HD, :] = refs[r][places.values(0, length)]
            values_ref[r, HD:, :] = jnp.ones((ONES, length), bf16)

    query = query_ref[turn]
    count = query.shape[1]
    peak = jnp.full((1, count), -jnp.inf, f32)
    mixed = jnp.zeros((HD + ONES, count), f32)
    spots = [(r, c) for r in range(chunks) for c in range(0, length, block)]

    def score(spot):
        r, c = spot
        return dot(keys_ref[r, c : c + block, :], query, NN)

    ahead = score(spots[0])
    for step, (r, c) in enumerate(spots):
        scores = ahead
        if step + 1 < len(spots):
            ahead = score(spots[step + 1])
        higher = jnp.maximum(peak, jnp.max(scores, axis=0, keepdims=True))
        expo = jnp.exp(scores - higher)
        shrink = jnp.exp(peak - higher)
        mixed = mixed * shrink + dot(values_ref[r, :, c : c + block], lower(expo), NN)
        peak = higher
    total = mixed[HD : HD + 1]
    out = lower(mixed[:HD] / total)
    for r in range(chunks):

        @pl.when(turn == r)
        def _():
            out_refs[r][...] = out

    lse_ref[0] = peak + jnp.log(total)


def attend_forward(sources, count):
    chunks = len(sources)
    places = Places(sources[0].shape, count)
    length = places.length
    block = math.gcd(length, 256)
    steps = chunks * chunks * count * length
    *outs, lse = pl.pallas_call(
        functools.partial(forward_kernel, chunks=chunks, block=block, places=places),
        grid=(chunks,),
        in_specs=[fixed(s.shape) for s in sources],
        out_specs=[fixed((HD, count))] * chunks + [pl.BlockSpec((1, 1, count), lambda i: (i, 0, 0))],
        out_shape=[jax.ShapeDtypeStruct((HD, count), bf16)] * chunks
        + [jax.ShapeDtypeStruct((chunks, 1, count), f32)],
        scratch_shapes=[
            pltpu.VMEM((chunks, HD, count), bf16),
            pltpu.VMEM((chunks, length, HD), bf16),
            pltpu.VMEM((chunks, HD + ONES, length), bf16),
        ],
        compiler_params=pltpu.CompilerParams(vmem_limit_bytes=VMEM),
        cost_estimate=pl.CostEstimate(
            flops=steps * 2 * 2 * 256, bytes_accessed=4 * chunks * length * 64, transcendentals=steps
        ),
        name="attend_forward",
    )(*sources)
    return outs, lse


def backward_kernel(*refs, chunks, block, places):
    refs, dout_refs, out_refs, refs_left = (
        refs[:chunks],
        refs[chunks : 2 * chunks],
        refs[2 * chunks : 3 * chunks],
        refs[3 * chunks :],
    )
    lse_ref, grads, scratch = refs_left[0], refs_left[1 : 1 + chunks], refs_left[1 + chunks :]
    query_ref, dout_ref, delta_ref, keys_ref, keys_acc, values_acc = scratch
    turn = pl.program_id(0)
    length = places.length

    @pl.when(turn == 0)
    def _():
        for r in range(chunks):
            keys_ref[r] = refs[r][places.keys(0, length)].T
            query_ref[r] = refs[r][places.query()] * jnp.asarray(SCALE, bf16)
            dout_ref[r] = dout_refs[r][...]
            delta_ref[r] = jnp.sum(
                widen(dout_refs[r][...]) * widen(out_refs[r][...]), axis=0, keepdims=True
            )
        keys_acc[...] = jnp.zeros_like(keys_acc)
        values_acc[...] = jnp.zeros_like(values_acc)

    query = query_ref[turn]
    dout = dout_ref[turn]
    count = query.shape[1]

    def across(row):
        if block % 128:
            return jnp.broadcast_to(row, (block, count)).T
        return jnp.concatenate([jnp.broadcast_to(row, (128, count)).T] * (block // 128), axis=1)

    lse_cols = across(lse_ref[0])
    delta_cols = across(delta_ref[turn])
    query_rows = query.T
    dout_rows = dout.T
    query_grad = jnp.zeros((count, HD), f32)
    spots = [(r, c) for r in range(chunks) for c in range(0, length, block)]

    def score(spot):
        r, c = spot
        return (
            dot(query_rows, refs[r][places.keys(c, c + block)], NN),
            dot(dout_rows, refs[r][places.values(c, c + block)], NN),
        )

    ahead = score(spots[0])
    for step, (r, c) in enumerate(spots):
        scores, prob_grad = ahead
        if step + 1 < len(spots):
            ahead = score(spots[step + 1])
        span = slice(c, c + block)
        probability = jnp.exp(scores - lse_cols)
        score_grad = lower(probability * (prob_grad - delta_cols))
        query_grad = query_grad + dot(score_grad, keys_ref[r, span, :], NN)
        values_acc[r, :, span] += dot(dout, lower(probability), NN)
        keys_acc[r, :, span] += dot(query, score_grad, NN)
    query_grad = lower((query_grad * SCALE).T)
    for r in range(chunks):

        @pl.when(turn == r)
        def _():
            grads[r][places.query()] = query_grad

    @pl.when(turn == chunks - 1)
    def _():
        for r in range(chunks):
            grads[r][places.keys(0, length)] = lower(keys_acc[r])
            grads[r][places.values(0, length)] = lower(values_acc[r])


def attend_backward(sources, douts, outs, lse):
    chunks = len(sources)
    count = douts[0].shape[1]
    places = Places(sources[0].shape, count)
    length = places.length
    block = math.gcd(length, 256)
    steps = chunks * chunks * count * length
    results = [s.shape for s in sources]
    sources = list(sources) + list(douts) + list(outs)
    return pl.pallas_call(
        functools.partial(backward_kernel, chunks=chunks, block=block, places=places),
        grid=(chunks,),
        in_specs=[fixed(s.shape) for s in sources] + [pl.BlockSpec((1, 1, count), lambda i: (i, 0, 0))],
        out_specs=[fixed(s) for s in results],
        out_shape=[jax.ShapeDtypeStruct(s, bf16) for s in results],
        scratch_shapes=[
            pltpu.VMEM((chunks, HD, count), bf16),
            pltpu.VMEM((chunks, HD, count), bf16),
            pltpu.VMEM((chunks, 1, count), f32),
            pltpu.VMEM((chunks, length, HD), bf16),
            pltpu.VMEM((chunks, HD, length), f32),
            pltpu.VMEM((chunks, HD, length), f32),
        ],
        compiler_params=pltpu.CompilerParams(vmem_limit_bytes=VMEM),
        cost_estimate=pl.CostEstimate(
            flops=steps * 2 * 5 * 200, bytes_accessed=8 * chunks * length * 64, transcendentals=steps
        ),
        name="attend_backward",
    )(*sources, lse)


def split_kernel(me_ref, source_ref, *out_refs, heads):
    turn = pl.program_id(0)
    for k in range(len(out_refs) // heads):

        @pl.when(turn == k)
        def _():
            for j in range(heads):
                out_refs[k * heads + j][...] = source_ref[0, j]


def split(values, me):
    chunks, heads, height, count = values.shape
    outs = pl.pallas_call(
        functools.partial(split_kernel, heads=heads),
        grid_spec=pltpu.PrefetchScalarGridSpec(
            num_scalar_prefetch=1,
            grid=(chunks,),
            in_specs=[pl.BlockSpec((1, heads, height, count), lambda k, m: (m[0] ^ k, 0, 0, 0))],
            out_specs=[fixed((height, count))] * (chunks * heads),
        ),
        out_shape=[jax.ShapeDtypeStruct((height, count), bf16)] * (chunks * heads),
        compiler_params=pltpu.CompilerParams(vmem_limit_bytes=VMEM),
        cost_estimate=pl.CostEstimate(flops=0, bytes_accessed=4 * values.size, transcendentals=0),
        name="split",
    )(me, values)
    return [[outs[k * heads + j] for k in range(chunks)] for j in range(heads)]


def split_pair_kernel(me_ref, query_ref, keyval_ref, *out_refs, heads):
    turn = pl.program_id(0)
    places = Places(out_refs[0].shape, query_ref.shape[3])
    length = places.length
    for k in range(len(out_refs) // heads):

        @pl.when(turn == k)
        def _():
            for j in range(heads):
                out_ref = out_refs[k * heads + j]
                out_ref[places.query()] = query_ref[0, j]
                out_ref[places.keys(0, length)] = keyval_ref[0, j, :HD, :]
                out_ref[places.values(0, length)] = keyval_ref[0, j, HD:, :]


def split_pair(queries, keyvals, me):
    chunks, heads, _, count = queries.shape
    length = keyvals.shape[3]
    shape = (HD, count + 2 * length)
    outs = pl.pallas_call(
        functools.partial(split_pair_kernel, heads=heads),
        grid_spec=pltpu.PrefetchScalarGridSpec(
            num_scalar_prefetch=1,
            grid=(chunks,),
            in_specs=[
                pl.BlockSpec((1, heads, HD, count), lambda k, m: (m[0] ^ k, 0, 0, 0)),
                pl.BlockSpec((1, heads, 2 * HD, length), lambda k, m: (m[0] ^ k, 0, 0, 0)),
            ],
            out_specs=[fixed(shape)] * (chunks * heads),
        ),
        out_shape=[jax.ShapeDtypeStruct(shape, bf16)] * (chunks * heads),
        compiler_params=pltpu.CompilerParams(vmem_limit_bytes=VMEM),
        cost_estimate=pl.CostEstimate(
            flops=0, bytes_accessed=4 * (queries.size + keyvals.size), transcendentals=0
        ),
        name="split_pair",
    )(me, queries, keyvals)
    return [[outs[k * heads + j] for k in range(chunks)] for j in range(heads)]


def assemble_pair_kernel(me_ref, *refs, heads):
    turn = pl.program_id(0)
    refs, (query_ref, keyval_ref) = refs[:-2], refs[-2:]
    places = Places(refs[0].shape, query_ref.shape[3])
    length = places.length
    for k in range(len(refs) // heads):

        @pl.when(turn == k)
        def _():
            for j in range(heads):
                source = refs[k * heads + j]
                query_ref[0, j] = source[places.query()]
                keyval_ref[0, j, :HD, :] = source[places.keys(0, length)]
                keyval_ref[0, j, HD:, :] = source[places.values(0, length)]


def assemble_pair(parts, me, count):
    heads, chunks = len(parts), len(parts[0])
    shape = parts[0][0].shape
    length = (shape[1] - count) // 2
    sources = [parts[j][k] for k in range(chunks) for j in range(heads)]
    return pl.pallas_call(
        functools.partial(assemble_pair_kernel, heads=heads),
        grid_spec=pltpu.PrefetchScalarGridSpec(
            num_scalar_prefetch=1,
            grid=(chunks,),
            in_specs=[fixed(shape)] * (chunks * heads),
            out_specs=[
                pl.BlockSpec((1, heads, HD, count), lambda k, m: (m[0] ^ k, 0, 0, 0)),
                pl.BlockSpec((1, heads, 2 * HD, length), lambda k, m: (m[0] ^ k, 0, 0, 0)),
            ],
        ),
        out_shape=[
            jax.ShapeDtypeStruct((chunks, heads, HD, count), bf16),
            jax.ShapeDtypeStruct((chunks, heads, 2 * HD, length), bf16),
        ],
        compiler_params=pltpu.CompilerParams(vmem_limit_bytes=VMEM),
        cost_estimate=pl.CostEstimate(
            flops=0, bytes_accessed=4 * chunks * heads * HD * shape[1], transcendentals=0
        ),
        name="assemble_pair",
    )(me, *sources)


def assemble_kernel(me_ref, *refs, heads):
    turn = pl.program_id(0)
    out_ref = refs[-1]
    for k in range((len(refs) - 1) // heads):

        @pl.when(turn == k)
        def _():
            for j in range(heads):
                out_ref[0, j] = refs[k * heads + j][...]


def assemble(parts, me):
    heads, chunks = len(parts), len(parts[0])
    height, count = parts[0][0].shape
    sources = [parts[j][k] for k in range(chunks) for j in range(heads)]
    return pl.pallas_call(
        functools.partial(assemble_kernel, heads=heads),
        grid_spec=pltpu.PrefetchScalarGridSpec(
            num_scalar_prefetch=1,
            grid=(chunks,),
            in_specs=[fixed((height, count))] * (chunks * heads),
            out_specs=pl.BlockSpec((1, heads, height, count), lambda k, m: (m[0] ^ k, 0, 0, 0)),
        ),
        out_shape=jax.ShapeDtypeStruct((chunks, heads, height, count), bf16),
        compiler_params=pltpu.CompilerParams(vmem_limit_bytes=VMEM),
        cost_estimate=pl.CostEstimate(
            flops=0, bytes_accessed=4 * chunks * heads * height * count, transcendentals=0
        ),
        name="assemble",
    )(me, *sources)


def tap_rows(cell_ref, frac_ref, live, plane, points):
    cell = cell_ref[0, plane : plane + 1, points]
    row = cell // (2 * G)
    col = cell - row * (2 * G)
    across = frac_ref[0, 2 * plane : 2 * plane + 1, points]
    downward = frac_ref[0, 2 * plane + 1 : 2 * plane + 2, points]
    half = lax.broadcasted_iota(jnp.int32, (G, cell.shape[1]), 0) * 2

    def spread(start, fraction, odd, gate):
        place = half + odd
        return jnp.where(
            place == start,
            (1.0 - fraction) * gate,
            jnp.where(place == start + 1, fraction * gate, 0.0),
        )

    return (
        [spread(row, downward, odd, live) for odd in range(2)],
        [spread(col, across, odd, 1.0) for odd in range(2)],
    )


def tap_table(table_ref, down, side):
    for ty in range(G):
        table_ref[ty * G : (ty + 1) * G, :] = lower(down[ty : ty + 1, :] * side)


def sample_kernel(
    object_ref, cell_ref, frac_ref, live_ref, chunk_ref, out_ref, table_ref, picked_ref, plane_ref, *, width
):
    turn = pl.program_id(1)

    @pl.when(turn == 0)
    def _():
        chunks = chunk_ref.shape[1]
        rows = TOK_OBJ // (2 * chunks)
        for r in range(chunks):
            for s in range(2):
                start = (s * chunks + r) * rows
                plane_ref[:, start : start + rows] = chunk_ref[0, r, :, s * rows : (s + 1) * rows]

    lanes = pl.ds(pl.multiple_of(turn * width, width), width)
    live = jnp.concatenate([live_ref[0]] * (width // RB), axis=1)
    picked = jnp.zeros((CH, width), f32)
    slot = 0
    for plane in range(3):
        downs, sides = tap_rows(cell_ref, frac_ref, live, plane, lanes)
        for dy in range(2):
            for dx in range(2):
                tap_table(table_ref.at[slot], downs[dy], sides[dx])
                part = (2 * dy + dx) * CH
                features = plane_ref[part : part + CH, plane * PIX : (plane + 1) * PIX]
                picked = picked + dot(features, table_ref[slot], NN)
                slot = 1 - slot
    picked_ref[:, lanes] = picked

    @pl.when(turn == pl.num_programs(1) - 1)
    def _():
        for s in range(out_ref.shape[1] // CH):
            out_ref[:, s * CH : (s + 1) * CH] = lower(picked_ref[:, s * RB : (s + 1) * RB].T)


def sample_points(planes, owner, cells, fractions, live):
    points = cells.shape[2]
    width = 512
    out = (RB, points // RB * CH)
    return pl.pallas_call(
        functools.partial(sample_kernel, width=width),
        grid_spec=pltpu.PrefetchScalarGridSpec(
            num_scalar_prefetch=1,
            grid=(1, points // width),
            in_specs=[
                fixed((1, 3, points)),
                fixed((1, 6, points)),
                fixed((1, 1, RB)),
                pl.BlockSpec((1,) + planes.shape[1:], lambda b, t, o: (o[b], 0, 0, 0)),
            ],
            out_specs=fixed(out),
            scratch_shapes=[
                pltpu.VMEM((2, PIX, width), bf16),
                pltpu.VMEM((CH, points), f32),
                pltpu.VMEM((4 * CH, TOK_OBJ), bf16),
            ],
        ),
        out_shape=jax.ShapeDtypeStruct(out, bf16),
        compiler_params=pltpu.CompilerParams(vmem_limit_bytes=VMEM),
        cost_estimate=pl.CostEstimate(
            flops=points * 3 * 4096 * 2 * 256, bytes_accessed=5 * 2**20, transcendentals=0
        ),
        name="sample_points",
    )(owner, cells, fractions, live, planes)


def scatter_kernel(object_ref, cell_ref, frac_ref, live_ref, grad_ref, out_ref, table_ref, rows_ref, total_ref, *, width):
    block = pl.program_id(0)
    turn = pl.program_id(1)
    owner = object_ref[block]

    @pl.when((block == 0) & (turn == 0))
    def _():
        total_ref[...] = jnp.zeros_like(total_ref)

    @pl.when(turn == 0)
    def _():
        for s in range(SAMP):
            rows_ref[:, s * RB : (s + 1) * RB] = grad_ref[:, s * CH : (s + 1) * CH].T

    lanes = pl.ds(pl.multiple_of(turn * width, width), width)
    live = jnp.concatenate([live_ref[0]] * (width // RB), axis=1)
    grads = rows_ref[:, lanes]
    slot = 0
    for plane in range(3):
        downs, sides = tap_rows(cell_ref, frac_ref, live, plane, lanes)
        for dy in range(2):
            for dx in range(2):
                tap_table(table_ref.at[slot], downs[dy], sides[dx])
                part = (2 * dy + dx) * CH
                total_ref[owner, part : part + CH, plane * PIX : (plane + 1) * PIX] += dot(
                    grads, table_ref[slot], NT
                )
                slot = 1 - slot

    @pl.when((block == pl.num_programs(0) - 1) & (turn == pl.num_programs(1) - 1))
    def _():
        objects, chunks = out_ref.shape[:2]
        rows = TOK_OBJ // (2 * chunks)
        for o in range(objects):
            for r in range(chunks):
                for s in range(2):
                    start = (s * chunks + r) * rows
                    out_ref[o, r, :, s * rows : (s + 1) * rows] = lower(
                        total_ref[o, :, start : start + rows]
                    )


def scatter_points(grads, owners, cells, fractions, live, objects, chunks):
    blocks = owners.shape[0]
    points = RB * SAMP
    width = 512
    shape = (objects, 4 * CH, TOK_OBJ)
    spread = (objects, chunks, 4 * CH, TOK_OBJ // chunks)
    return pl.pallas_call(
        functools.partial(scatter_kernel, width=width),
        grid_spec=pltpu.PrefetchScalarGridSpec(
            num_scalar_prefetch=1,
            grid=(blocks, points // width),
            in_specs=[
                pl.BlockSpec((1, 3, points), lambda b, t, o: (b, 0, 0)),
                pl.BlockSpec((1, 6, points), lambda b, t, o: (b, 0, 0)),
                pl.BlockSpec((1, 1, RB), lambda b, t, o: (b, 0, 0)),
                pl.BlockSpec((RB, SAMP * CH), lambda b, t, o: (b, 0)),
            ],
            out_specs=fixed(spread),
            scratch_shapes=[
                pltpu.VMEM((2, PIX, width), bf16),
                pltpu.VMEM((CH, points), bf16),
                pltpu.VMEM(shape, f32),
            ],
        ),
        out_shape=jax.ShapeDtypeStruct(spread, bf16),
        compiler_params=pltpu.CompilerParams(vmem_limit_bytes=VMEM),
        cost_estimate=pl.CostEstimate(
            flops=blocks * points * 3 * 4096 * 2 * 256,
            bytes_accessed=blocks * 5 * 2**20,
            transcendentals=0,
        ),
        name="scatter_points",
    )(owners, cells, fractions, live, grads)


SWAP = [(0, 1), (1, 0)]


def body(
    dp_axes,
    group_axes,
    tokens,
    dino,
    first_gain,
    first_shift,
    image_weight,
    cross_query,
    cross_keyval,
    cross_output,
    second_gain,
    second_shift,
    self_project,
    self_output,
    third_gain,
    third_shift,
    hidden_weight,
    hidden_bias,
    output_weight,
    deconv_weight,
    ray_mask,
    block_object,
    sample_cell,
    sample_frac,
    out_grad,
    sampled_grad,
):
    shard_axes = ("h",) + group_axes
    every = dp_axes + shard_axes
    outer, core = dp_axes
    group = 2 ** len(group_axes)
    heads = H // group
    half = lax.axis_index("h")
    side = lax.axis_index(core)
    over = lax.axis_index(outer)
    place = lax.axis_index(group_axes)
    me = place.reshape(1).astype(jnp.int32)
    rows = tokens.shape[0]
    count = 2 * rows
    patches = 2 * dino.shape[0]
    share = first_gain.shape[0]
    join = lax.optimization_barrier

    def own_object(values):
        mine = lax.dynamic_index_in_dim(values, half, 1, keepdims=False)
        other = lax.dynamic_index_in_dim(values, 1 - half, 1, keepdims=False)
        got = lax.ppermute(other, "h", SWAP)
        return jnp.concatenate(
            [jnp.where(half == 0, mine, got), jnp.where(half == 0, got, mine)], axis=0
        )

    def gather(pieces):
        return lax.all_gather(jnp.concatenate(pieces, axis=1), every, axis=0, tiled=True)

    def exchange(chunks):
        return [chunks[0]] + [
            lax.ppermute(chunks[k], group_axes, [(i, i ^ k) for i in range(group)])
            for k in range(1, group)
        ]

    def after(values, *other):
        return join((values, other))[0]

    def in_turn(call, *lists):
        done = []
        for operands in zip(*lists):
            done.append(call(*(after(operands, done[-1]) if done else operands)))
        return done

    def exchange_all(parts):
        done = []
        for chunks in parts:
            if done:
                chunks, done[-1] = join((chunks, done[-1]))
            done.append(exchange(chunks))
        return done

    columns = jnp.stack(
        [first_gain, first_shift, second_gain, second_shift, third_gain, third_shift], axis=1
    )
    columns = jnp.concatenate([columns, hidden_bias.reshape(share, FF // D)], axis=1)
    columns = jnp.pad(columns, ((0, 0), (0, 128 - columns.shape[1])))
    early = gather(
        [
            lower(cross_query),
            lower(cross_keyval),
            lower(image_weight).reshape(share, DINO),
            lower(columns),
        ]
    )
    query_w = early[:, :D]
    keyval_w = early[:, D : 3 * D]
    image_w = early[:, 3 * D : 3 * D + DINO].reshape(DINO, D)
    vectors = widen(early[:, 3 * D + DINO :])
    gain_a, shift_a, gain_b, shift_b, gain_c, shift_c = [vectors[:, i] for i in range(6)]
    bias = vectors[:, 6 : 6 + FF // D].reshape(FF)

    blocks = ray_mask.shape[0] // RB

    def by_sample(values):
        kinds = values.shape[0]
        values = values.reshape(kinds, blocks, RB, SAMP)
        return values.transpose(1, 0, 3, 2).reshape(blocks, kinds, SAMP * RB)

    cells = by_sample(sample_cell)
    fractions = by_sample(sample_frac)
    live = widen(ray_mask).reshape(blocks, 1, RB)
    plane_grad = scatter_points(sampled_grad, block_object, cells, fractions, live, 2, group)
    token_low = own_object(tokens)
    dino_values = own_object(dino)
    plane_grad, token_low, dino_values = join((plane_grad, token_low, dino_values))
    plane_low = lax.psum_scatter(
        plane_grad.reshape(2 * group * 4 * CH, count), shard_axes, scatter_dimension=0, tiled=True
    )
    token_values = widen(token_low)

    normed_full, unit_a, inverse_a = normalize(token_values, gain_a, shift_a)
    normed_a = lower(normed_full)
    image = lower(dot(dino_values, image_w, NN))
    queries = lower(dot(query_w, normed_a, ((0,), (1,)))).reshape(group, heads, HD, count)
    keyvals = lower(dot(keyval_w, image, ((0,), (1,)))).reshape(group, heads, 2 * HD, patches)
    cross_in = exchange_all(split_pair(queries, keyvals, me))
    middle = [lower(cross_output), lower(self_project), lower(self_output)]
    late = [lower(hidden_weight), lower(deconv_weight)]
    output_w = lower(output_weight)
    middle, late = gather(middle), gather(late)
    output_w = lax.all_gather(output_w, every, axis=0, tiled=True)
    cross_w = middle[:, :D]
    project_w = middle[:, D : 4 * D]
    self_w = middle[:, 4 * D :]
    hidden_w = late[:, :FF]
    deconv_w = late[:, FF:]
    cross_out = in_turn(lambda x: attend_forward(x, count), cross_in)
    cross_mix = assemble([exchange(o) for o, _ in cross_out], me).reshape(D, count)
    after_cross = token_values + dot(cross_mix, cross_w, TN)

    normed_full, unit_b, inverse_b = normalize(after_cross, gain_b, shift_b)
    normed_b = lower(normed_full)
    projected = lower(dot(project_w, normed_b, ((0,), (1,)))).reshape(group, heads, 3 * HD, count)
    projected, out_grad = join((split(projected, me), out_grad))
    out_cotangent = own_object(out_grad)
    self_qkv = exchange_all(projected)
    self_out = in_turn(lambda x: attend_forward(x, count), self_qkv)
    out_cotangent = after(out_cotangent, self_out[-1])
    self_mix = assemble([exchange(o) for o, _ in self_out], me).reshape(D, count)
    after_self = after_cross + dot(self_mix, self_w, TN)

    normed_full, unit_c, inverse_c = normalize(after_self, gain_c, shift_c)
    normed_c = lower(normed_full)
    hidden = dot(normed_c, hidden_w, NN) + bias
    activated = lower(gelu(hidden))
    result_low = lower(after_self + dot(activated, output_w, NN))

    planes = lower(dot(deconv_w, result_low, ((0,), (1,))))
    plane_all = lax.all_gather(planes, shard_axes, axis=0, tiled=True)
    plane_all = plane_all.reshape(2, group, 4 * CH, count)


    def grad_job(left, axis, right, right_axis, pieces=1):
        quarter = left.shape[axis] // 4
        dims = ((1 - axis,), (right_axis,))

        def block(y, c):
            return lax.dynamic_slice_in_dim(left, (2 * y + c) * quarter, quarter, axis)

        def blocks_of(c):
            parts = [block(1 - over, c), block(over, c)]
            return parts if quarter > 512 else [jnp.concatenate(parts, axis=axis)]

        others = [lower(dot(x, right, dims)) for x in blocks_of(1 - side)]
        others = yield (), [(x, core) for x in others]
        sums = [lower(dot(x, right, dims) + widen(g)) for x, g in zip(blocks_of(side), others)]
        away, kept = sums if quarter > 512 else (sums[0][:quarter], sums[0][quarter:])
        width = away.shape[1] // pieces
        got = []
        for i in range(pieces):
            got += yield kept, [(away[:, i * width : (i + 1) * width], outer)]
        return lower(widen(kept) + widen(jnp.concatenate(got, axis=1) if pieces > 1 else got[0]))

    def chain_job(values):
        left = list(shard_axes)
        values = [v.reshape((2,) * len(left) + (-1, v.shape[-1])) for v in values]
        for axis in group_axes[::-1] + ("h",):
            dim, here = left.index(axis), lax.axis_index(axis)
            left.pop(dim)
            away = [lax.dynamic_index_in_dim(v, 1 - here, dim, keepdims=False) for v in values]
            kept = [lax.dynamic_index_in_dim(v, here, dim, keepdims=False) for v in values]
            got = yield kept, [(x, axis) for x in away]
            values = [widen(k) + widen(g) for k, g in zip(kept, got)]
            if left:
                values = [lower(v) for v in values]
        return values

    def full_job(*args):
        part = yield from grad_job(*args)
        return (yield from chain_job([part]))[0]

    def together(runs):
        results, got = [None] * len(runs), [None] * len(runs)
        left = list(range(len(runs)))
        while True:
            kept, sent, sizes = [], [], []
            for i in list(left):
                try:
                    stand, moves = next(runs[i]) if got[i] is None else runs[i].send(got[i])
                except StopIteration as end:
                    results[i] = end.value
                    left.remove(i)
                    continue
                kept.append(stand)
                sent += moves
                sizes.append(len(moves))
            if not left:
                return results
            arrived = yield kept, sent
            for i, size in zip(left, sizes):
                got[i], arrived = arrived[:size], arrived[size:]

    def side_job(*runs):
        parts = yield from together(runs)
        return (yield from chain_job([jnp.concatenate(parts, axis=1)]))[0]

    def swap_job(arrays, pieces):
        done = []
        for values in arrays:
            size = values.shape[0] // 2
            step = size // pieces
            mine = lax.dynamic_slice_in_dim(values, half * size, size, 0)
            away = lower(lax.dynamic_slice_in_dim(values, (1 - half) * size, size, 0))
            got = []
            for i in range(pieces):
                got += yield done, [(away[i * step : (i + 1) * step], "h")]
            got = jnp.concatenate(got, axis=0).astype(mine.dtype)
            done.append(
                jnp.stack([jnp.where(half == 0, mine, got), jnp.where(half == 0, got, mine)], axis=1)
            )
        return done

    jobs, sums_of = {}, {}

    def turn(call, operands):
        kept, sent = {}, {}
        for name in list(jobs):
            job, got = jobs[name]
            try:
                kept[name], sent[name] = next(job) if got is None else job.send(got)
            except StopIteration as end:
                sums_of[name] = end.value
                del jobs[name]
        arrays = {name: [x for x, _ in sent[name]] for name in sent}
        operands, arrays, _ = join((operands, arrays, kept))
        moved = {
            name: [lax.ppermute(x, axis, SWAP) for x, (_, axis) in zip(arrays[name], sent[name])]
            for name in sent
        }
        raw = call(*operands)
        moved, settled = join((moved, raw))
        for name in sent:
            jobs[name] = (jobs[name][0], moved[name])
        return raw, settled

    def start(name, job):
        jobs[name] = (job, None)

    result_grad = widen(out_cotangent) + dot(plane_low, deconv_w, ((0,), (1,)))
    result_low_grad = lower(result_grad)
    activated_grad = dot(result_low_grad, output_w, NT)
    _, gelu_pull = jax.vjp(gelu, hidden)
    hidden_grad = lower(gelu_pull(activated_grad)[0])
    bias_grad = jnp.sum(widen(hidden_grad), axis=0)
    back_c, gain_c_grad, shift_c_grad = normalize_back(
        dot(hidden_grad, hidden_w, NT), unit_c, inverse_c, gain_c
    )
    self_grad = result_grad + back_c

    self_low = lower(self_grad)
    self_mix_grad = lower(dot(self_w, self_low, NT)).reshape(group, heads, HD, count)
    self_dout = exchange_all(split(self_mix_grad, me))
    start("output", full_job(activated, 1, result_low_grad, 0, 2))
    gone = ()
    self_back = []
    for j in range(heads):
        if j == min(2, heads - 1):
            start("hidden", full_job(normed_c, 1, hidden_grad, 0, 2))
            start("self", full_job(self_mix, 0, self_low, 0))
            start("deconv", full_job(result_low, 1, plane_low, 1))
        if j == min(1, heads - 1):
            start("tokens_out", swap_job([result_low], 4))
        raw, gone = turn(
            lambda s, g, o: attend_backward(s, g, *o),
            (after(self_qkv[j], gone), self_dout[j], self_out[j]),
        )
        self_back.append(raw)

    project_grad = assemble([exchange(g) for g in self_back], me).reshape(3 * D, count)
    back_b, gain_b_grad, shift_b_grad = normalize_back(
        dot(project_grad, project_w, ((0,), (1,))), unit_b, inverse_b, gain_b
    )
    cross_grad = self_grad + back_b

    cross_low = lower(cross_grad)
    cross_mix_grad = lower(dot(cross_w, cross_low, NT)).reshape(group, heads, HD, count)
    cross_dout = exchange_all(split(cross_mix_grad, me))
    start(
        "project",
        side_job(grad_job(normed_b, 1, project_grad, 1, 2), grad_job(cross_mix, 0, cross_low, 0)),
    )
    cut = heads // 2
    cross_back, parts, found = [], [], []

    def kv_grads(first, last):
        queries, keyvals = assemble_pair(parts[first:last], me, count)
        queries = queries.reshape(-1, count)
        keyvals = keyvals.reshape(-1, patches)
        start(f"keyval{first}", grad_job(image, 1, keyvals, 1))
        start(f"query{first}", grad_job(normed_a, 1, queries, 1))
        found.append((queries, keyvals))

    for j in range(heads):
        if cut and j == cut + 1:
            parts[:cut] = after(parts[:cut], gone)
            kv_grads(0, cut)
        raw, gone = turn(
            lambda s, g, o: attend_backward(s, g, *o),
            (after(cross_in[j], gone), cross_dout[j], cross_out[j]),
        )
        cross_back.append(raw)
        parts.append(exchange(raw))

    pieces = [(b, s) for b in range(blocks) for s in range(2)]
    span = SAMP * RB // 2
    sampled = {}

    def sample_turn(gone):
        b, s = pieces[len(sampled)]
        operands = (
            plane_all,
            block_object[b : b + 1],
            cells[b : b + 1, :, s * span : (s + 1) * span],
            fractions[b : b + 1, :, s * span : (s + 1) * span],
            live[b : b + 1],
        )
        _, sampled[b, s] = turn(sample_points, after(operands, gone))
        return sampled[b, s]

    gone = sample_turn(gone)
    parts[cut:] = after(parts[cut:], gone)
    kv_grads(cut, heads)

    def merge(pieces, height):
        folded = [p.reshape(group, -1, height, p.shape[-1]) for p in pieces]
        return jnp.concatenate(folded, axis=1).reshape(-1, pieces[0].shape[-1])

    def merge_columns(pieces, height):
        folded = [p.reshape(p.shape[0], group, -1, height) for p in pieces]
        return jnp.concatenate(folded, axis=2).reshape(pieces[0].shape[0], -1)

    query_back = merge([f[0] for f in found], HD)
    keyval_back = merge([f[1] for f in found], 2 * HD)
    image_grad = lower(dot(keyval_back, keyval_w, ((0,), (1,))))
    start("image", grad_job(dino_values, 1, image_grad, 0))
    back_a, gain_a_grad, shift_a_grad = normalize_back(
        dot(query_back, query_w, ((0,), (1,))), unit_a, inverse_a, gain_a
    )
    dino_grad = dot(image_grad, image_w, NT)
    tokens_grad = cross_grad + back_a

    sums = jnp.stack(
        [gain_a_grad, shift_a_grad, gain_b_grad, shift_b_grad, gain_c_grad, shift_c_grad], axis=1
    )
    sums = jnp.concatenate([sums, bias_grad.reshape(D, FF // D)], axis=1)
    sums = jnp.pad(sums, ((0, 0), (0, 128 - sums.shape[1])))

    def vector_job():
        def quarter_rows(y, c):
            return lax.dynamic_slice_in_dim(sums, (2 * y + c) * (D // 4), D // 4, 0)

        others = yield (), [(quarter_rows(y, 1 - side), core) for y in (1 - over, over)]
        away = quarter_rows(1 - over, side) + others[0]
        kept = quarter_rows(over, side) + others[1]
        got = yield kept, [(away, outer)]
        return lower(kept + got[0])

    start("vectors", vector_job())
    (dino_grad, tokens_grad), gone = join(((dino_grad, tokens_grad), gone))
    start("swap", swap_job([dino_grad, tokens_grad], 2))
    gone = sample_turn(gone)
    gone = sample_turn(gone)
    names = [f"{kind}{at}" for at in ([0, cut] if cut else [0]) for kind in ("keyval", "query")]
    names += ["vectors", "image"]
    while any(name in jobs for name in names):
        _, gone = turn(lambda *x: x, (gone,))
    last_part = jnp.concatenate([sums_of[name] for name in names[:-1]], axis=1)
    start("last", chain_job([last_part, sums_of["image"]]))
    gone = sample_turn(gone)
    while jobs:
        _, gone = turn(lambda *x: x, (gone,))
    last, image_sum = sums_of["last"]
    dino_grad, tokens_grad = sums_of["swap"]
    (tokens_out,) = sums_of["tokens_out"]
    sampled = jnp.concatenate(
        [jnp.concatenate([sampled[b, s] for s in range(2)], axis=1) for b in range(blocks)], axis=0
    )

    keyval_sums, query_sums = [], []
    at = 0
    for width in [group * n * HD for n in ([cut, heads - cut] if cut else [heads])]:
        keyval_sums.append(last[:, at : at + 2 * width])
        query_sums.append(last[:, at + 2 * width : at + 3 * width])
        at += 3 * width
    vector_sums = last[:, at:]

    return (
        tokens_out,
        sampled,
        tokens_grad,
        dino_grad,
        vector_sums[:, 0],
        vector_sums[:, 1],
        image_sum,
        merge_columns(query_sums, HD),
        merge_columns(keyval_sums, 2 * HD),
        sums_of["project"][:, 3 * D :],
        vector_sums[:, 2],
        vector_sums[:, 3],
        sums_of["project"][:, : 3 * D],
        sums_of["self"],
        vector_sums[:, 4],
        vector_sums[:, 5],
        sums_of["hidden"],
        vector_sums[:, 6 : 6 + FF // D].reshape(share * (FF // D)),
        sums_of["output"],
        sums_of["deconv"],
    )


def solution(mesh):
    dp_bits = mesh.shape["dp"].bit_length() - 1
    shard_bits = mesh.shape["shard"].bit_length() - 1
    dp_axes = tuple(f"d{i}" for i in range(dp_bits))
    group_axes = tuple(f"r{i}" for i in range(shard_bits - 1))
    shard_axes = ("h",) + group_axes
    fine = Mesh(mesh.devices.reshape((2,) * (dp_bits + shard_bits)), dp_axes + shard_axes)
    every = dp_axes + shard_axes
    rows = P(shard_axes, dp_axes, None)
    vector = P(every)
    matrix = P(every, None)
    points = P(None, every)
    return jax.shard_map(
        functools.partial(body, dp_axes, group_axes),
        mesh=fine,
        in_specs=(
            rows, rows,
            vector, vector, matrix, matrix, matrix, matrix,
            vector, vector, matrix, matrix,
            vector, vector, matrix, vector, matrix, matrix,
            vector, vector, points, points, rows, matrix,
        ),
        out_specs=(
            rows, matrix, rows, rows,
            vector, vector, matrix, matrix, matrix, matrix,
            vector, vector, matrix, matrix,
            vector, vector, matrix, vector, matrix, matrix,
        ),
        check_vma=False,
    )
```

```python
import functools
import math

import jax
import jax.numpy as jnp
from jax import lax
from jax.experimental import pallas as pl
from jax.experimental.pallas import tpu as pltpu
from jax.sharding import Mesh
from jax.sharding import PartitionSpec as P

D = 1024
H = 16
HD = 64
FF = 4096
DINO = 768
CH = 80
G = 32
RB = 128
SAMP = 32
TOK_OBJ = 3072
PIX = G * G
SCALE = HD ** (-0.5)
VMEM = 58 * 2**20
ONES = 16

epsilon = 1e-05
NN = ((1,), (0,))
NT = ((1,), (1,))
TN = ((0,), (0,))
bf16 = jnp.bfloat16
f32 = jnp.float32


def lower(value):
    return value.astype(bf16)


def widen(value):
    return value.astype(f32)


def dot(left, right, dims):
    return lax.dot_general(left, right, (dims, ((), ())), preferred_element_type=f32)


def normalize(values, gain, shift):
    centered = values - jnp.mean(values, axis=-1, keepdims=True)
    inverse = lax.rsqrt(jnp.mean(centered * centered, axis=-1, keepdims=True) + epsilon)
    unit = centered * inverse
    return (unit * gain + shift, unit, inverse)


def normalize_back(grad, unit, inverse, gain):
    gain_grad = jnp.sum(grad * unit, axis=0)
    shift_grad = jnp.sum(grad, axis=0)
    scaled = grad * gain
    inner = (
        scaled
        - jnp.mean(scaled, axis=-1, keepdims=True)
        - unit * jnp.mean(scaled * unit, axis=-1, keepdims=True)
    )
    return (inverse * inner, gain_grad, shift_grad)


def gelu(values):
    return 0.5 * values * (1.0 + lax.erf(values * 0.7071067811865476))


def fixed(shape):
    return pl.BlockSpec(shape, lambda *_: (0,) * len(shape))


class Places:
    def __init__(self, shape, count):
        self.beside = shape[0] == HD
        self.count = count
        self.length = (shape[1] - count) // 2 if self.beside else shape[1]

    def query(self):
        return (slice(0, HD), slice(0, self.count))

    def keys(self, start, stop):
        if self.beside:
            return (slice(0, HD), slice(self.count + start, self.count + stop))
        return (slice(HD, 2 * HD), slice(start, stop))

    def values(self, start, stop):
        if self.beside:
            return self.keys(self.length + start, self.length + stop)
        return (slice(2 * HD, 3 * HD), slice(start, stop))


def forward_kernel(*refs, chunks, block, places):
    refs, out_refs = refs[:chunks], refs[chunks:]
    out_refs, (lse_ref, query_ref, keys_ref, values_ref) = out_refs[:chunks], out_refs[chunks:]
    turn = pl.program_id(0)
    length = places.length

    @pl.when(turn == 0)
    def _():
        for r in range(chunks):
            keys_ref[r] = refs[r][places.keys(0, length)].T
            query_ref[r] = refs[r][places.query()] * jnp.asarray(SCALE, bf16)
            values_ref[r, :HD, :] = refs[r][places.values(0, length)]
            values_ref[r, HD:, :] = jnp.ones((ONES, length), bf16)

    query = query_ref[turn]
    count = query.shape[1]
    peak = jnp.full((1, count), -jnp.inf, f32)
    mixed = jnp.zeros((HD + ONES, count), f32)
    spots = [(r, c) for r in range(chunks) for c in range(0, length, block)]

    def score(spot):
        r, c = spot
        return dot(keys_ref[r, c : c + block, :], query, NN)

    ahead = score(spots[0])
    for step, (r, c) in enumerate(spots):
        scores = ahead
        if step + 1 < len(spots):
            ahead = score(spots[step + 1])
        higher = jnp.maximum(peak, jnp.max(scores, axis=0, keepdims=True))
        expo = jnp.exp(scores - higher)
        shrink = jnp.exp(peak - higher)
        mixed = mixed * shrink + dot(values_ref[r, :, c : c + block], lower(expo), NN)
        peak = higher
    total = mixed[HD : HD + 1]
    out = lower(mixed[:HD] / total)
    for r in range(chunks):

        @pl.when(turn == r)
        def _():
            out_refs[r][...] = out

    lse_ref[0] = peak + jnp.log(total)


def attend_forward(sources, count):
    chunks = len(sources)
    places = Places(sources[0].shape, count)
    length = places.length
    block = math.gcd(length, 256)
    steps = chunks * chunks * count * length
    *outs, lse = pl.pallas_call(
        functools.partial(forward_kernel, chunks=chunks, block=block, places=places),
        grid=(chunks,),
        in_specs=[fixed(s.shape) for s in sources],
        out_specs=[fixed((HD, count))] * chunks + [pl.BlockSpec((1, 1, count), lambda i: (i, 0, 0))],
        out_shape=[jax.ShapeDtypeStruct((HD, count), bf16)] * chunks
        + [jax.ShapeDtypeStruct((chunks, 1, count), f32)],
        scratch_shapes=[
            pltpu.VMEM((chunks, HD, count), bf16),
            pltpu.VMEM((chunks, length, HD), bf16),
            pltpu.VMEM((chunks, HD + ONES, length), bf16),
        ],
        compiler_params=pltpu.CompilerParams(vmem_limit_bytes=VMEM),
        cost_estimate=pl.CostEstimate(
            flops=steps * 2 * 2 * 256, bytes_accessed=4 * chunks * length * 64, transcendentals=steps
        ),
        name="attend_forward",
    )(*sources)
    return outs, lse


def backward_kernel(*refs, chunks, block, places):
    refs, dout_refs, out_refs, refs_left = (
        refs[:chunks],
        refs[chunks : 2 * chunks],
        refs[2 * chunks : 3 * chunks],
        refs[3 * chunks :],
    )
    lse_ref, grads, scratch = refs_left[0], refs_left[1 : 1 + chunks], refs_left[1 + chunks :]
    query_ref, dout_ref, delta_ref, keys_ref, keys_acc, values_acc = scratch
    turn = pl.program_id(0)
    length = places.length

    @pl.when(turn == 0)
    def _():
        for r in range(chunks):
            keys_ref[r] = refs[r][places.keys(0, length)].T
            query_ref[r] = refs[r][places.query()] * jnp.asarray(SCALE, bf16)
            dout_ref[r] = dout_refs[r][...]
            delta_ref[r] = jnp.sum(
                widen(dout_refs[r][...]) * widen(out_refs[r][...]), axis=0, keepdims=True
            )
        keys_acc[...] = jnp.zeros_like(keys_acc)
        values_acc[...] = jnp.zeros_like(values_acc)

    query = query_ref[turn]
    dout = dout_ref[turn]
    count = query.shape[1]

    def across(row):
        if block % 128:
            return jnp.broadcast_to(row, (block, count)).T
        return jnp.concatenate([jnp.broadcast_to(row, (128, count)).T] * (block // 128), axis=1)

    lse_cols = across(lse_ref[0])
    delta_cols = across(delta_ref[turn])
    query_rows = query.T
    dout_rows = dout.T
    query_grad = jnp.zeros((count, HD), f32)
    spots = [(r, c) for r in range(chunks) for c in range(0, length, block)]

    def score(spot):
        r, c = spot
        return (
            dot(query_rows, refs[r][places.keys(c, c + block)], NN),
            dot(dout_rows, refs[r][places.values(c, c + block)], NN),
        )

    ahead = score(spots[0])
    for step, (r, c) in enumerate(spots):
        scores, prob_grad = ahead
        if step + 1 < len(spots):
            ahead = score(spots[step + 1])
        span = slice(c, c + block)
        probability = jnp.exp(scores - lse_cols)
        score_grad = lower(probability * (prob_grad - delta_cols))
        query_grad = query_grad + dot(score_grad, keys_ref[r, span, :], NN)
        values_acc[r, :, span] += dot(dout, lower(probability), NN)
        keys_acc[r, :, span] += dot(query, score_grad, NN)
    query_grad = lower((query_grad * SCALE).T)
    for r in range(chunks):

        @pl.when(turn == r)
        def _():
            grads[r][places.query()] = query_grad

    @pl.when(turn == chunks - 1)
    def _():
        for r in range(chunks):
            grads[r][places.keys(0, length)] = lower(keys_acc[r])
            grads[r][places.values(0, length)] = lower(values_acc[r])


def attend_backward(sources, douts, outs, lse):
    chunks = len(sources)
    count = douts[0].shape[1]
    places = Places(sources[0].shape, count)
    length = places.length
    block = math.gcd(length, 256)
    steps = chunks * chunks * count * length
    results = [s.shape for s in sources]
    sources = list(sources) + list(douts) + list(outs)
    return pl.pallas_call(
        functools.partial(backward_kernel, chunks=chunks, block=block, places=places),
        grid=(chunks,),
        in_specs=[fixed(s.shape) for s in sources] + [pl.BlockSpec((1, 1, count), lambda i: (i, 0, 0))],
        out_specs=[fixed(s) for s in results],
        out_shape=[jax.ShapeDtypeStruct(s, bf16) for s in results],
        scratch_shapes=[
            pltpu.VMEM((chunks, HD, count), bf16),
            pltpu.VMEM((chunks, HD, count), bf16),
            pltpu.VMEM((chunks, 1, count), f32),
            pltpu.VMEM((chunks, length, HD), bf16),
            pltpu.VMEM((chunks, HD, length), f32),
            pltpu.VMEM((chunks, HD, length), f32),
        ],
        compiler_params=pltpu.CompilerParams(vmem_limit_bytes=VMEM),
        cost_estimate=pl.CostEstimate(
            flops=steps * 2 * 5 * 200, bytes_accessed=8 * chunks * length * 64, transcendentals=steps
        ),
        name="attend_backward",
    )(*sources, lse)


def split_kernel(me_ref, source_ref, *out_refs, heads):
    turn = pl.program_id(0)
    for k in range(len(out_refs) // heads):

        @pl.when(turn == k)
        def _():
            for j in range(heads):
                out_refs[k * heads + j][...] = source_ref[0, j]


def split(values, me):
    chunks, heads, height, count = values.shape
    outs = pl.pallas_call(
        functools.partial(split_kernel, heads=heads),
        grid_spec=pltpu.PrefetchScalarGridSpec(
            num_scalar_prefetch=1,
            grid=(chunks,),
            in_specs=[pl.BlockSpec((1, heads, height, count), lambda k, m: (m[0] ^ k, 0, 0, 0))],
            out_specs=[fixed((height, count))] * (chunks * heads),
        ),
        out_shape=[jax.ShapeDtypeStruct((height, count), bf16)] * (chunks * heads),
        compiler_params=pltpu.CompilerParams(vmem_limit_bytes=VMEM),
        cost_estimate=pl.CostEstimate(flops=0, bytes_accessed=4 * values.size, transcendentals=0),
        name="split",
    )(me, values)
    return [[outs[k * heads + j] for k in range(chunks)] for j in range(heads)]


def split_pair_kernel(me_ref, query_ref, keyval_ref, *out_refs, heads):
    turn = pl.program_id(0)
    places = Places(out_refs[0].shape, query_ref.shape[3])
    length = places.length
    for k in range(len(out_refs) // heads):

        @pl.when(turn == k)
        def _():
            for j in range(heads):
                out_ref = out_refs[k * heads + j]
                out_ref[places.query()] = query_ref[0, j]
                out_ref[places.keys(0, length)] = keyval_ref[0, j, :HD, :]
                out_ref[places.values(0, length)] = keyval_ref[0, j, HD:, :]


def split_pair(queries, keyvals, me):
    chunks, heads, _, count = queries.shape
    length = keyvals.shape[3]
    shape = (HD, count + 2 * length)
    outs = pl.pallas_call(
        functools.partial(split_pair_kernel, heads=heads),
        grid_spec=pltpu.PrefetchScalarGridSpec(
            num_scalar_prefetch=1,
            grid=(chunks,),
            in_specs=[
                pl.BlockSpec((1, heads, HD, count), lambda k, m: (m[0] ^ k, 0, 0, 0)),
                pl.BlockSpec((1, heads, 2 * HD, length), lambda k, m: (m[0] ^ k, 0, 0, 0)),
            ],
            out_specs=[fixed(shape)] * (chunks * heads),
        ),
        out_shape=[jax.ShapeDtypeStruct(shape, bf16)] * (chunks * heads),
        compiler_params=pltpu.CompilerParams(vmem_limit_bytes=VMEM),
        cost_estimate=pl.CostEstimate(
            flops=0, bytes_accessed=4 * (queries.size + keyvals.size), transcendentals=0
        ),
        name="split_pair",
    )(me, queries, keyvals)
    return [[outs[k * heads + j] for k in range(chunks)] for j in range(heads)]


def assemble_pair_kernel(me_ref, *refs, heads):
    turn = pl.program_id(0)
    refs, (query_ref, keyval_ref) = refs[:-2], refs[-2:]
    places = Places(refs[0].shape, query_ref.shape[3])
    length = places.length
    for k in range(len(refs) // heads):

        @pl.when(turn == k)
        def _():
            for j in range(heads):
                source = refs[k * heads + j]
                query_ref[0, j] = source[places.query()]
                keyval_ref[0, j, :HD, :] = source[places.keys(0, length)]
                keyval_ref[0, j, HD:, :] = source[places.values(0, length)]


def assemble_pair(parts, me, count):
    heads, chunks = len(parts), len(parts[0])
    shape = parts[0][0].shape
    length = (shape[1] - count) // 2
    sources = [parts[j][k] for k in range(chunks) for j in range(heads)]
    return pl.pallas_call(
        functools.partial(assemble_pair_kernel, heads=heads),
        grid_spec=pltpu.PrefetchScalarGridSpec(
            num_scalar_prefetch=1,
            grid=(chunks,),
            in_specs=[fixed(shape)] * (chunks * heads),
            out_specs=[
                pl.BlockSpec((1, heads, HD, count), lambda k, m: (m[0] ^ k, 0, 0, 0)),
                pl.BlockSpec((1, heads, 2 * HD, length), lambda k, m: (m[0] ^ k, 0, 0, 0)),
            ],
        ),
        out_shape=[
            jax.ShapeDtypeStruct((chunks, heads, HD, count), bf16),
            jax.ShapeDtypeStruct((chunks, heads, 2 * HD, length), bf16),
        ],
        compiler_params=pltpu.CompilerParams(vmem_limit_bytes=VMEM),
        cost_estimate=pl.CostEstimate(
            flops=0, bytes_accessed=4 * chunks * heads * HD * shape[1], transcendentals=0
        ),
        name="assemble_pair",
    )(me, *sources)


def assemble_kernel(me_ref, *refs, heads):
    turn = pl.program_id(0)
    out_ref = refs[-1]
    for k in range((len(refs) - 1) // heads):

        @pl.when(turn == k)
        def _():
            for j in range(heads):
                out_ref[0, j] = refs[k * heads + j][...]


def assemble(parts, me):
    heads, chunks = len(parts), len(parts[0])
    height, count = parts[0][0].shape
    sources = [parts[j][k] for k in range(chunks) for j in range(heads)]
    return pl.pallas_call(
        functools.partial(assemble_kernel, heads=heads),
        grid_spec=pltpu.PrefetchScalarGridSpec(
            num_scalar_prefetch=1,
            grid=(chunks,),
            in_specs=[fixed((height, count))] * (chunks * heads),
            out_specs=pl.BlockSpec((1, heads, height, count), lambda k, m: (m[0] ^ k, 0, 0, 0)),
        ),
        out_shape=jax.ShapeDtypeStruct((chunks, heads, height, count), bf16),
        compiler_params=pltpu.CompilerParams(vmem_limit_bytes=VMEM),
        cost_estimate=pl.CostEstimate(
            flops=0, bytes_accessed=4 * chunks * heads * height * count, transcendentals=0
        ),
        name="assemble",
    )(me, *sources)


def tap_rows(cell_ref, frac_ref, live, plane, points):
    cell = cell_ref[0, plane : plane + 1, points]
    row = cell // (2 * G)
    col = cell - row * (2 * G)
    across = frac_ref[0, 2 * plane : 2 * plane + 1, points]
    downward = frac_ref[0, 2 * plane + 1 : 2 * plane + 2, points]
    half = lax.broadcasted_iota(jnp.int32, (G, cell.shape[1]), 0) * 2

    def spread(start, fraction, odd, gate):
        place = half + odd
        return jnp.where(
            place == start,
            (1.0 - fraction) * gate,
            jnp.where(place == start + 1, fraction * gate, 0.0),
        )

    return (
        [spread(row, downward, odd, live) for odd in range(2)],
        [spread(col, across, odd, 1.0) for odd in range(2)],
    )


def tap_table(table_ref, down, side):
    for ty in range(G):
        table_ref[ty * G : (ty + 1) * G, :] = lower(down[ty : ty + 1, :] * side)


def sample_kernel(
    object_ref, cell_ref, frac_ref, live_ref, chunk_ref, out_ref, table_ref, picked_ref, plane_ref, *, width
):
    turn = pl.program_id(1)

    @pl.when(turn == 0)
    def _():
        chunks = chunk_ref.shape[1]
        rows = TOK_OBJ // (2 * chunks)
        for r in range(chunks):
            for s in range(2):
                start = (s * chunks + r) * rows
                plane_ref[:, start : start + rows] = chunk_ref[0, r, :, s * rows : (s + 1) * rows]

    lanes = pl.ds(pl.multiple_of(turn * width, width), width)
    live = jnp.concatenate([live_ref[0]] * (width // RB), axis=1)
    picked = jnp.zeros((CH, width), f32)
    slot = 0
    for plane in range(3):
        downs, sides = tap_rows(cell_ref, frac_ref, live, plane, lanes)
        for dy in range(2):
            for dx in range(2):
                tap_table(table_ref.at[slot], downs[dy], sides[dx])
                part = (2 * dy + dx) * CH
                features = plane_ref[part : part + CH, plane * PIX : (plane + 1) * PIX]
                picked = picked + dot(features, table_ref[slot], NN)
                slot = 1 - slot
    picked_ref[:, lanes] = picked

    @pl.when(turn == pl.num_programs(1) - 1)
    def _():
        for s in range(out_ref.shape[1] // CH):
            out_ref[:, s * CH : (s + 1) * CH] = lower(picked_ref[:, s * RB : (s + 1) * RB].T)


def sample_points(planes, owner, cells, fractions, live):
    points = cells.shape[2]
    width = 512
    out = (RB, points // RB * CH)
    return pl.pallas_call(
        functools.partial(sample_kernel, width=width),
        grid_spec=pltpu.PrefetchScalarGridSpec(
            num_scalar_prefetch=1,
            grid=(1, points // width),
            in_specs=[
                fixed((1, 3, points)),
                fixed((1, 6, points)),
                fixed((1, 1, RB)),
                pl.BlockSpec((1,) + planes.shape[1:], lambda b, t, o: (o[b], 0, 0, 0)),
            ],
            out_specs=fixed(out),
            scratch_shapes=[
                pltpu.VMEM((2, PIX, width), bf16),
                pltpu.VMEM((CH, points), f32),
                pltpu.VMEM((4 * CH, TOK_OBJ), bf16),
            ],
        ),
        out_shape=jax.ShapeDtypeStruct(out, bf16),
        compiler_params=pltpu.CompilerParams(vmem_limit_bytes=VMEM),
        cost_estimate=pl.CostEstimate(
            flops=points * 3 * 4096 * 2 * 256, bytes_accessed=5 * 2**20, transcendentals=0
        ),
        name="sample_points",
    )(owner, cells, fractions, live, planes)


def scatter_kernel(object_ref, cell_ref, frac_ref, live_ref, grad_ref, out_ref, table_ref, rows_ref, total_ref, *, width):
    block = pl.program_id(0)
    turn = pl.program_id(1)
    owner = object_ref[block]

    @pl.when((block == 0) & (turn == 0))
    def _():
        total_ref[...] = jnp.zeros_like(total_ref)

    @pl.when(turn == 0)
    def _():
        for s in range(SAMP):
            rows_ref[:, s * RB : (s + 1) * RB] = grad_ref[:, s * CH : (s + 1) * CH].T

    lanes = pl.ds(pl.multiple_of(turn * width, width), width)
    live = jnp.concatenate([live_ref[0]] * (width // RB), axis=1)
    grads = rows_ref[:, lanes]
    slot = 0
    for plane in range(3):
        downs, sides = tap_rows(cell_ref, frac_ref, live, plane, lanes)
        for dy in range(2):
            for dx in range(2):
                tap_table(table_ref.at[slot], downs[dy], sides[dx])
                part = (2 * dy + dx) * CH
                total_ref[owner, part : part + CH, plane * PIX : (plane + 1) * PIX] += dot(
                    grads, table_ref[slot], NT
                )
                slot = 1 - slot

    @pl.when((block == pl.num_programs(0) - 1) & (turn == pl.num_programs(1) - 1))
    def _():
        objects, chunks = out_ref.shape[:2]
        rows = TOK_OBJ // (2 * chunks)
        for o in range(objects):
            for r in range(chunks):
                for s in range(2):
                    start = (s * chunks + r) * rows
                    out_ref[o, r, :, s * rows : (s + 1) * rows] = lower(
                        total_ref[o, :, start : start + rows]
                    )


def scatter_points(grads, owners, cells, fractions, live, objects, chunks):
    blocks = owners.shape[0]
    points = RB * SAMP
    width = 512
    shape = (objects, 4 * CH, TOK_OBJ)
    spread = (objects, chunks, 4 * CH, TOK_OBJ // chunks)
    return pl.pallas_call(
        functools.partial(scatter_kernel, width=width),
        grid_spec=pltpu.PrefetchScalarGridSpec(
            num_scalar_prefetch=1,
            grid=(blocks, points // width),
            in_specs=[
                pl.BlockSpec((1, 3, points), lambda b, t, o: (b, 0, 0)),
                pl.BlockSpec((1, 6, points), lambda b, t, o: (b, 0, 0)),
                pl.BlockSpec((1, 1, RB), lambda b, t, o: (b, 0, 0)),
                pl.BlockSpec((RB, SAMP * CH), lambda b, t, o: (b, 0)),
            ],
            out_specs=fixed(spread),
            scratch_shapes=[
                pltpu.VMEM((2, PIX, width), bf16),
                pltpu.VMEM((CH, points), bf16),
                pltpu.VMEM(shape, f32),
            ],
        ),
        out_shape=jax.ShapeDtypeStruct(spread, bf16),
        compiler_params=pltpu.CompilerParams(vmem_limit_bytes=VMEM),
        cost_estimate=pl.CostEstimate(
            flops=blocks * points * 3 * 4096 * 2 * 256,
            bytes_accessed=blocks * 5 * 2**20,
            transcendentals=0,
        ),
        name="scatter_points",
    )(owners, cells, fractions, live, grads)


SWAP = [(0, 1), (1, 0)]


def body(
    dp_axes,
    group_axes,
    tokens,
    dino,
    first_gain,
    first_shift,
    image_weight,
    cross_query,
    cross_keyval,
    cross_output,
    second_gain,
    second_shift,
    self_project,
    self_output,
    third_gain,
    third_shift,
    hidden_weight,
    hidden_bias,
    output_weight,
    deconv_weight,
    ray_mask,
    block_object,
    sample_cell,
    sample_frac,
    out_grad,
    sampled_grad,
):
    shard_axes = ("h",) + group_axes
    every = dp_axes + shard_axes
    outer, core = dp_axes
    group = 2 ** len(group_axes)
    heads = H // group
    half = lax.axis_index("h")
    side = lax.axis_index(core)
    over = lax.axis_index(outer)
    place = lax.axis_index(group_axes)
    me = place.reshape(1).astype(jnp.int32)
    rows = tokens.shape[0]
    count = 2 * rows
    patches = 2 * dino.shape[0]
    share = first_gain.shape[0]
    join = lax.optimization_barrier

    def own_object(values):
        mine = lax.dynamic_index_in_dim(values, half, 1, keepdims=False)
        other = lax.dynamic_index_in_dim(values, 1 - half, 1, keepdims=False)
        got = lax.ppermute(other, "h", SWAP)
        return jnp.concatenate(
            [jnp.where(half == 0, mine, got), jnp.where(half == 0, got, mine)], axis=0
        )

    def gather(pieces):
        return lax.all_gather(jnp.concatenate(pieces, axis=1), every, axis=0, tiled=True)

    def exchange(chunks):
        return [chunks[0]] + [
            lax.ppermute(chunks[k], group_axes, [(i, i ^ k) for i in range(group)])
            for k in range(1, group)
        ]

    def after(values, *other):
        return join((values, other))[0]

    def in_turn(call, *lists):
        done = []
        for operands in zip(*lists):
            done.append(call(*(after(operands, done[-1]) if done else operands)))
        return done

    def exchange_all(parts):
        done = []
        for chunks in parts:
            if done:
                chunks, done[-1] = join((chunks, done[-1]))
            done.append(exchange(chunks))
        return done

    columns = jnp.stack(
        [first_gain, first_shift, second_gain, second_shift, third_gain, third_shift], axis=1
    )
    columns = jnp.concatenate([columns, hidden_bias.reshape(share, FF // D)], axis=1)
    columns = jnp.pad(columns, ((0, 0), (0, 128 - columns.shape[1])))
    early = gather(
        [
            lower(cross_query),
            lower(cross_keyval),
            lower(image_weight).reshape(share, DINO),
            lower(columns),
        ]
    )
    query_w = early[:, :D]
    keyval_w = early[:, D : 3 * D]
    image_w = early[:, 3 * D : 3 * D + DINO].reshape(DINO, D)
    vectors = widen(early[:, 3 * D + DINO :])
    gain_a, shift_a, gain_b, shift_b, gain_c, shift_c = [vectors[:, i] for i in range(6)]
    bias = vectors[:, 6 : 6 + FF // D].reshape(FF)

    blocks = ray_mask.shape[0] // RB

    def by_sample(values):
        kinds = values.shape[0]
        values = values.reshape(kinds, blocks, RB, SAMP)
        return values.transpose(1, 0, 3, 2).reshape(blocks, kinds, SAMP * RB)

    cells = by_sample(sample_cell)
    fractions = by_sample(sample_frac)
    live = widen(ray_mask).reshape(blocks, 1, RB)
    plane_grad = scatter_points(sampled_grad, block_object, cells, fractions, live, 2, group)
    token_low = own_object(tokens)
    dino_values = own_object(dino)
    plane_grad, token_low, dino_values = join((plane_grad, token_low, dino_values))
    plane_low = lax.psum_scatter(
        plane_grad.reshape(2 * group * 4 * CH, count), shard_axes, scatter_dimension=0, tiled=True
    )
    token_values = widen(token_low)

    normed_full, unit_a, inverse_a = normalize(token_values, gain_a, shift_a)
    normed_a = lower(normed_full)
    image = lower(dot(dino_values, image_w, NN))
    queries = lower(dot(query_w, normed_a, ((0,), (1,)))).reshape(group, heads, HD, count)
    keyvals = lower(dot(keyval_w, image, ((0,), (1,)))).reshape(group, heads, 2 * HD, patches)
    cross_in = exchange_all(split_pair(queries, keyvals, me))
    middle = [lower(cross_output), lower(self_project), lower(self_output)]
    late = [lower(hidden_weight), lower(deconv_weight)]
    output_w = lower(output_weight)
    middle, late = gather(middle), gather(late)
    output_w = lax.all_gather(output_w, every, axis=0, tiled=True)
    cross_w = middle[:, :D]
    project_w = middle[:, D : 4 * D]
    self_w = middle[:, 4 * D :]
    hidden_w = late[:, :FF]
    deconv_w = late[:, FF:]
    cross_out = in_turn(lambda x: attend_forward(x, count), cross_in)
    cross_mix = assemble([exchange(o) for o, _ in cross_out], me).reshape(D, count)
    after_cross = token_values + dot(cross_mix, cross_w, TN)

    normed_full, unit_b, inverse_b = normalize(after_cross, gain_b, shift_b)
    normed_b = lower(normed_full)
    projected = lower(dot(project_w, normed_b, ((0,), (1,)))).reshape(group, heads, 3 * HD, count)
    projected, out_grad = join((split(projected, me), out_grad))
    out_cotangent = own_object(out_grad)
    self_qkv = exchange_all(projected)
    self_out = in_turn(lambda x: attend_forward(x, count), self_qkv)
    out_cotangent = after(out_cotangent, self_out[-1])
    self_mix = assemble([exchange(o) for o, _ in self_out], me).reshape(D, count)
    after_self = after_cross + dot(self_mix, self_w, TN)

    normed_full, unit_c, inverse_c = normalize(after_self, gain_c, shift_c)
    normed_c = lower(normed_full)
    hidden = dot(normed_c, hidden_w, NN) + bias
    activated = lower(gelu(hidden))
    result_low = lower(after_self + dot(activated, output_w, NN))

    planes = lower(dot(deconv_w, result_low, ((0,), (1,))))
    plane_all = lax.all_gather(planes, shard_axes, axis=0, tiled=True)
    plane_all = plane_all.reshape(2, group, 4 * CH, count)


    def grad_job(left, axis, right, right_axis, pieces=1):
        quarter = left.shape[axis] // 4
        dims = ((1 - axis,), (right_axis,))

        def block(y, c):
            part = lax.dynamic_slice_in_dim(left, (2 * y + c) * quarter, quarter, axis)
            return dot(part, right, dims)

        others = [lower(block(y, 1 - side)) for y in (1 - over, over)]
        others = yield (), [(x, core) for x in others]
        away = lower(block(1 - over, side) + widen(others[0]))
        kept = lower(block(over, side) + widen(others[1]))
        width = away.shape[1] // pieces
        got = []
        for i in range(pieces):
            got += yield kept, [(away[:, i * width : (i + 1) * width], outer)]
        return lower(widen(kept) + widen(jnp.concatenate(got, axis=1) if pieces > 1 else got[0]))

    def chain_job(values):
        left = list(shard_axes)
        values = [v.reshape((2,) * len(left) + (-1, v.shape[-1])) for v in values]
        for axis in group_axes[::-1] + ("h",):
            dim, here = left.index(axis), lax.axis_index(axis)
            left.pop(dim)
            away = [lax.dynamic_index_in_dim(v, 1 - here, dim, keepdims=False) for v in values]
            kept = [lax.dynamic_index_in_dim(v, here, dim, keepdims=False) for v in values]
            got = yield kept, [(x, axis) for x in away]
            values = [widen(k) + widen(g) for k, g in zip(kept, got)]
            if left:
                values = [lower(v) for v in values]
        return values

    def full_job(*args):
        part = yield from grad_job(*args)
        return (yield from chain_job([part]))[0]

    def swap_job(arrays, pieces):
        done = []
        for values in arrays:
            size = values.shape[0] // 2
            step = size // pieces
            mine = lax.dynamic_slice_in_dim(values, half * size, size, 0)
            away = lower(lax.dynamic_slice_in_dim(values, (1 - half) * size, size, 0))
            got = []
            for i in range(pieces):
                got += yield done, [(away[i * step : (i + 1) * step], "h")]
            got = jnp.concatenate(got, axis=0).astype(mine.dtype)
            done.append(
                jnp.stack([jnp.where(half == 0, mine, got), jnp.where(half == 0, got, mine)], axis=1)
            )
        return done

    jobs, sums_of = {}, {}

    def turn(call, operands):
        kept, sent = {}, {}
        for name in list(jobs):
            job, got = jobs[name]
            try:
                kept[name], sent[name] = next(job) if got is None else job.send(got)
            except StopIteration as end:
                sums_of[name] = end.value
                del jobs[name]
        arrays = {name: [x for x, _ in sent[name]] for name in sent}
        operands, arrays, _ = join((operands, arrays, kept))
        moved = {
            name: [lax.ppermute(x, axis, SWAP) for x, (_, axis) in zip(arrays[name], sent[name])]
            for name in sent
        }
        raw = call(*operands)
        moved, settled = join((moved, raw))
        for name in sent:
            jobs[name] = (jobs[name][0], moved[name])
        return raw, settled

    def start(name, job):
        jobs[name] = (job, None)

    result_grad = widen(out_cotangent) + dot(plane_low, deconv_w, ((0,), (1,)))
    result_low_grad = lower(result_grad)
    activated_grad = dot(result_low_grad, output_w, NT)
    _, gelu_pull = jax.vjp(gelu, hidden)
    hidden_grad = lower(gelu_pull(activated_grad)[0])
    bias_grad = jnp.sum(widen(hidden_grad), axis=0)
    back_c, gain_c_grad, shift_c_grad = normalize_back(
        dot(hidden_grad, hidden_w, NT), unit_c, inverse_c, gain_c
    )
    self_grad = result_grad + back_c

    self_low = lower(self_grad)
    self_mix_grad = lower(dot(self_w, self_low, NT)).reshape(group, heads, HD, count)
    self_dout = exchange_all(split(self_mix_grad, me))
    start("output", full_job(activated, 1, result_low_grad, 0, 2))
    gone = ()
    self_back = []
    for j in range(heads):
        if j == min(2, heads - 1):
            start("hidden", full_job(normed_c, 1, hidden_grad, 0, 2))
            start("self", full_job(self_mix, 0, self_low, 0, 1))
            start("deconv", full_job(result_low, 1, plane_low, 1, 1))
        if j == min(1, heads - 1):
            start("tokens_out", swap_job([result_low], 4))
        raw, gone = turn(
            lambda s, g, o: attend_backward(s, g, *o),
            (after(self_qkv[j], gone), self_dout[j], self_out[j]),
        )
        self_back.append(raw)

    project_grad = assemble([exchange(g) for g in self_back], me).reshape(3 * D, count)
    back_b, gain_b_grad, shift_b_grad = normalize_back(
        dot(project_grad, project_w, ((0,), (1,))), unit_b, inverse_b, gain_b
    )
    cross_grad = self_grad + back_b

    cross_low = lower(cross_grad)
    cross_mix_grad = lower(dot(cross_w, cross_low, NT)).reshape(group, heads, HD, count)
    cross_dout = exchange_all(split(cross_mix_grad, me))
    start("project", full_job(normed_b, 1, project_grad, 1, 2))
    start("cross", full_job(cross_mix, 0, cross_low, 0, 1))
    cut = heads // 2
    cross_back, parts, found = [], [], []

    def kv_grads(first, last):
        queries, keyvals = assemble_pair(parts[first:last], me, count)
        queries = queries.reshape(-1, count)
        keyvals = keyvals.reshape(-1, patches)
        start(f"keyval{first}", grad_job(image, 1, keyvals, 1))
        start(f"query{first}", grad_job(normed_a, 1, queries, 1))
        found.append((queries, keyvals))

    for j in range(heads):
        if cut and j == cut + 1:
            parts[:cut] = after(parts[:cut], gone)
            kv_grads(0, cut)
        raw, gone = turn(
            lambda s, g, o: attend_backward(s, g, *o),
            (after(cross_in[j], gone), cross_dout[j], cross_out[j]),
        )
        cross_back.append(raw)
        parts.append(exchange(raw))

    pieces = [(b, s) for b in range(blocks) for s in range(2)]
    span = SAMP * RB // 2
    sampled = {}

    def sample_turn(gone):
        b, s = pieces[len(sampled)]
        operands = (
            plane_all,
            block_object[b : b + 1],
            cells[b : b + 1, :, s * span : (s + 1) * span],
            fractions[b : b + 1, :, s * span : (s + 1) * span],
            live[b : b + 1],
        )
        _, sampled[b, s] = turn(sample_points, after(operands, gone))
        return sampled[b, s]

    gone = sample_turn(gone)
    parts[cut:] = after(parts[cut:], gone)
    kv_grads(cut, heads)

    def merge(pieces, height):
        folded = [p.reshape(group, -1, height, p.shape[-1]) for p in pieces]
        return jnp.concatenate(folded, axis=1).reshape(-1, pieces[0].shape[-1])

    def merge_columns(pieces, height):
        folded = [p.reshape(p.shape[0], group, -1, height) for p in pieces]
        return jnp.concatenate(folded, axis=2).reshape(pieces[0].shape[0], -1)

    query_back = merge([f[0] for f in found], HD)
    keyval_back = merge([f[1] for f in found], 2 * HD)
    image_grad = lower(dot(keyval_back, keyval_w, ((0,), (1,))))
    start("image", grad_job(dino_values, 1, image_grad, 0))
    back_a, gain_a_grad, shift_a_grad = normalize_back(
        dot(query_back, query_w, ((0,), (1,))), unit_a, inverse_a, gain_a
    )
    dino_grad = dot(image_grad, image_w, NT)
    tokens_grad = cross_grad + back_a

    sums = jnp.stack(
        [gain_a_grad, shift_a_grad, gain_b_grad, shift_b_grad, gain_c_grad, shift_c_grad], axis=1
    )
    sums = jnp.concatenate([sums, bias_grad.reshape(D, FF // D)], axis=1)
    sums = jnp.pad(sums, ((0, 0), (0, 128 - sums.shape[1])))

    def vector_job():
        def quarter_rows(y, c):
            return lax.dynamic_slice_in_dim(sums, (2 * y + c) * (D // 4), D // 4, 0)

        others = yield (), [(quarter_rows(y, 1 - side), core) for y in (1 - over, over)]
        away = quarter_rows(1 - over, side) + others[0]
        kept = quarter_rows(over, side) + others[1]
        got = yield kept, [(away, outer)]
        return lower(kept + got[0])

    start("vectors", vector_job())
    (dino_grad, tokens_grad), gone = join(((dino_grad, tokens_grad), gone))
    start("swap", swap_job([dino_grad, tokens_grad], 2))
    gone = sample_turn(gone)
    gone = sample_turn(gone)
    names = [f"{kind}{at}" for at in ([0, cut] if cut else [0]) for kind in ("keyval", "query")]
    names += ["vectors", "image"]
    while any(name in jobs for name in names):
        _, gone = turn(lambda *x: x, (gone,))
    last_part = jnp.concatenate([sums_of[name] for name in names[:-1]], axis=1)
    start("last", chain_job([last_part, sums_of["image"]]))
    gone = sample_turn(gone)
    while jobs:
        _, gone = turn(lambda *x: x, (gone,))
    last, image_sum = sums_of["last"]
    dino_grad, tokens_grad = sums_of["swap"]
    (tokens_out,) = sums_of["tokens_out"]
    sampled = jnp.concatenate(
        [jnp.concatenate([sampled[b, s] for s in range(2)], axis=1) for b in range(blocks)], axis=0
    )

    keyval_sums, query_sums = [], []
    at = 0
    for width in [group * n * HD for n in ([cut, heads - cut] if cut else [heads])]:
        keyval_sums.append(last[:, at : at + 2 * width])
        query_sums.append(last[:, at + 2 * width : at + 3 * width])
        at += 3 * width
    vector_sums = last[:, at:]

    return (
        tokens_out,
        sampled,
        tokens_grad,
        dino_grad,
        vector_sums[:, 0],
        vector_sums[:, 1],
        image_sum,
        merge_columns(query_sums, HD),
        merge_columns(keyval_sums, 2 * HD),
        sums_of["cross"],
        vector_sums[:, 2],
        vector_sums[:, 3],
        sums_of["project"],
        sums_of["self"],
        vector_sums[:, 4],
        vector_sums[:, 5],
        sums_of["hidden"],
        vector_sums[:, 6 : 6 + FF // D].reshape(share * (FF // D)),
        sums_of["output"],
        sums_of["deconv"],
    )


def solution(mesh):
    dp_bits = mesh.shape["dp"].bit_length() - 1
    shard_bits = mesh.shape["shard"].bit_length() - 1
    dp_axes = tuple(f"d{i}" for i in range(dp_bits))
    group_axes = tuple(f"r{i}" for i in range(shard_bits - 1))
    shard_axes = ("h",) + group_axes
    fine = Mesh(mesh.devices.reshape((2,) * (dp_bits + shard_bits)), dp_axes + shard_axes)
    every = dp_axes + shard_axes
    rows = P(shard_axes, dp_axes, None)
    vector = P(every)
    matrix = P(every, None)
    points = P(None, every)
    return jax.shard_map(
        functools.partial(body, dp_axes, group_axes),
        mesh=fine,
        in_specs=(
            rows, rows,
            vector, vector, matrix, matrix, matrix, matrix,
            vector, vector, matrix, matrix,
            vector, vector, matrix, vector, matrix, matrix,
            vector, vector, points, points, rows, matrix,
        ),
        out_specs=(
            rows, matrix, rows, rows,
            vector, vector, matrix, matrix, matrix, matrix,
            vector, vector, matrix, matrix,
            vector, vector, matrix, vector, matrix, matrix,
        ),
        check_vma=False,
    )
```

```python
import functools
import math

import jax
import jax.numpy as jnp
from jax import lax
from jax.experimental import pallas as pl
from jax.experimental.pallas import tpu as pltpu
from jax.sharding import Mesh
from jax.sharding import PartitionSpec as P

D = 1024
H = 16
HD = 64
FF = 4096
DINO = 768
CH = 80
G = 32
RB = 128
SAMP = 32
TOK_OBJ = 3072
PIX = G * G
SCALE = HD ** (-0.5)
VMEM = 58 * 2**20
ONES = 16

epsilon = 1e-05
NN = ((1,), (0,))
NT = ((1,), (1,))
TN = ((0,), (0,))
bf16 = jnp.bfloat16
f32 = jnp.float32


def lower(value):
    return value.astype(bf16)


def widen(value):
    return value.astype(f32)


def dot(left, right, dims):
    return lax.dot_general(left, right, (dims, ((), ())), preferred_element_type=f32)


def normalize(values, gain, shift):
    centered = values - jnp.mean(values, axis=-1, keepdims=True)
    inverse = lax.rsqrt(jnp.mean(centered * centered, axis=-1, keepdims=True) + epsilon)
    unit = centered * inverse
    return (unit * gain + shift, unit, inverse)


def normalize_back(grad, unit, inverse, gain):
    gain_grad = jnp.sum(grad * unit, axis=0)
    shift_grad = jnp.sum(grad, axis=0)
    scaled = grad * gain
    inner = (
        scaled
        - jnp.mean(scaled, axis=-1, keepdims=True)
        - unit * jnp.mean(scaled * unit, axis=-1, keepdims=True)
    )
    return (inverse * inner, gain_grad, shift_grad)


def gelu(values):
    return 0.5 * values * (1.0 + lax.erf(values * 0.7071067811865476))


def fixed(shape):
    return pl.BlockSpec(shape, lambda *_: (0,) * len(shape))


class Places:
    def __init__(self, shape, count):
        self.beside = shape[0] == HD
        self.count = count
        self.length = (shape[1] - count) // 2 if self.beside else shape[1]

    def query(self):
        return (slice(0, HD), slice(0, self.count))

    def keys(self, start, stop):
        if self.beside:
            return (slice(0, HD), slice(self.count + start, self.count + stop))
        return (slice(HD, 2 * HD), slice(start, stop))

    def values(self, start, stop):
        if self.beside:
            return self.keys(self.length + start, self.length + stop)
        return (slice(2 * HD, 3 * HD), slice(start, stop))


def forward_kernel(*refs, chunks, block, places):
    refs, out_refs = refs[:chunks], refs[chunks:]
    out_refs, (lse_ref, query_ref, keys_ref, values_ref) = out_refs[:chunks], out_refs[chunks:]
    turn = pl.program_id(0)
    length = places.length

    @pl.when(turn == 0)
    def _():
        for r in range(chunks):
            keys_ref[r] = refs[r][places.keys(0, length)].T
            query_ref[r] = refs[r][places.query()] * jnp.asarray(SCALE, bf16)
            values_ref[r, :HD, :] = refs[r][places.values(0, length)]
            values_ref[r, HD:, :] = jnp.ones((ONES, length), bf16)

    query = query_ref[turn]
    count = query.shape[1]
    peak = jnp.full((1, count), -jnp.inf, f32)
    mixed = jnp.zeros((HD + ONES, count), f32)
    spots = [(r, c) for r in range(chunks) for c in range(0, length, block)]

    def score(spot):
        r, c = spot
        return dot(keys_ref[r, c : c + block, :], query, NN)

    ahead = score(spots[0])
    for step, (r, c) in enumerate(spots):
        scores = ahead
        if step + 1 < len(spots):
            ahead = score(spots[step + 1])
        higher = jnp.maximum(peak, jnp.max(scores, axis=0, keepdims=True))
        expo = jnp.exp(scores - higher)
        shrink = jnp.exp(peak - higher)
        mixed = mixed * shrink + dot(values_ref[r, :, c : c + block], lower(expo), NN)
        peak = higher
    total = mixed[HD : HD + 1]
    out = lower(mixed[:HD] / total)
    for r in range(chunks):

        @pl.when(turn == r)
        def _():
            out_refs[r][...] = out

    lse_ref[0] = peak + jnp.log(total)


def attend_forward(sources, count):
    chunks = len(sources)
    places = Places(sources[0].shape, count)
    length = places.length
    block = math.gcd(length, 256)
    steps = chunks * chunks * count * length
    *outs, lse = pl.pallas_call(
        functools.partial(forward_kernel, chunks=chunks, block=block, places=places),
        grid=(chunks,),
        in_specs=[fixed(s.shape) for s in sources],
        out_specs=[fixed((HD, count))] * chunks + [pl.BlockSpec((1, 1, count), lambda i: (i, 0, 0))],
        out_shape=[jax.ShapeDtypeStruct((HD, count), bf16)] * chunks
        + [jax.ShapeDtypeStruct((chunks, 1, count), f32)],
        scratch_shapes=[
            pltpu.VMEM((chunks, HD, count), bf16),
            pltpu.VMEM((chunks, length, HD), bf16),
            pltpu.VMEM((chunks, HD + ONES, length), bf16),
        ],
        compiler_params=pltpu.CompilerParams(vmem_limit_bytes=VMEM),
        cost_estimate=pl.CostEstimate(
            flops=steps * 2 * 2 * 256, bytes_accessed=4 * chunks * length * 64, transcendentals=steps
        ),
        name="attend_forward",
    )(*sources)
    return outs, lse


def backward_kernel(*refs, chunks, block, places):
    refs, dout_refs, out_refs, refs_left = (
        refs[:chunks],
        refs[chunks : 2 * chunks],
        refs[2 * chunks : 3 * chunks],
        refs[3 * chunks :],
    )
    lse_ref, grads, scratch = refs_left[0], refs_left[1 : 1 + chunks], refs_left[1 + chunks :]
    query_ref, dout_ref, delta_ref, keys_ref, keys_acc, values_acc = scratch
    turn = pl.program_id(0)
    length = places.length

    @pl.when(turn == 0)
    def _():
        for r in range(chunks):
            keys_ref[r] = refs[r][places.keys(0, length)].T
            query_ref[r] = refs[r][places.query()] * jnp.asarray(SCALE, bf16)
            dout_ref[r] = dout_refs[r][...]
            delta_ref[r] = jnp.sum(
                widen(dout_refs[r][...]) * widen(out_refs[r][...]), axis=0, keepdims=True
            )
        keys_acc[...] = jnp.zeros_like(keys_acc)
        values_acc[...] = jnp.zeros_like(values_acc)

    query = query_ref[turn]
    dout = dout_ref[turn]
    count = query.shape[1]

    def across(row):
        if block % 128:
            return jnp.broadcast_to(row, (block, count)).T
        return jnp.concatenate([jnp.broadcast_to(row, (128, count)).T] * (block // 128), axis=1)

    lse_cols = across(lse_ref[0])
    delta_cols = across(delta_ref[turn])
    query_rows = query.T
    dout_rows = dout.T
    query_grad = jnp.zeros((count, HD), f32)
    spots = [(r, c) for r in range(chunks) for c in range(0, length, block)]

    def score(spot):
        r, c = spot
        return (
            dot(query_rows, refs[r][places.keys(c, c + block)], NN),
            dot(dout_rows, refs[r][places.values(c, c + block)], NN),
        )

    ahead = score(spots[0])
    for step, (r, c) in enumerate(spots):
        scores, prob_grad = ahead
        if step + 1 < len(spots):
            ahead = score(spots[step + 1])
        span = slice(c, c + block)
        probability = jnp.exp(scores - lse_cols)
        score_grad = lower(probability * (prob_grad - delta_cols))
        query_grad = query_grad + dot(score_grad, keys_ref[r, span, :], NN)
        values_acc[r, :, span] += dot(dout, lower(probability), NN)
        keys_acc[r, :, span] += dot(query, score_grad, NN)
    query_grad = lower((query_grad * SCALE).T)
    for r in range(chunks):

        @pl.when(turn == r)
        def _():
            grads[r][places.query()] = query_grad

    @pl.when(turn == chunks - 1)
    def _():
        for r in range(chunks):
            grads[r][places.keys(0, length)] = lower(keys_acc[r])
            grads[r][places.values(0, length)] = lower(values_acc[r])


def attend_backward(sources, douts, outs, lse):
    chunks = len(sources)
    count = douts[0].shape[1]
    places = Places(sources[0].shape, count)
    length = places.length
    block = math.gcd(length, 256)
    steps = chunks * chunks * count * length
    results = [s.shape for s in sources]
    sources = list(sources) + list(douts) + list(outs)
    return pl.pallas_call(
        functools.partial(backward_kernel, chunks=chunks, block=block, places=places),
        grid=(chunks,),
        in_specs=[fixed(s.shape) for s in sources] + [pl.BlockSpec((1, 1, count), lambda i: (i, 0, 0))],
        out_specs=[fixed(s) for s in results],
        out_shape=[jax.ShapeDtypeStruct(s, bf16) for s in results],
        scratch_shapes=[
            pltpu.VMEM((chunks, HD, count), bf16),
            pltpu.VMEM((chunks, HD, count), bf16),
            pltpu.VMEM((chunks, 1, count), f32),
            pltpu.VMEM((chunks, length, HD), bf16),
            pltpu.VMEM((chunks, HD, length), f32),
            pltpu.VMEM((chunks, HD, length), f32),
        ],
        compiler_params=pltpu.CompilerParams(vmem_limit_bytes=VMEM),
        cost_estimate=pl.CostEstimate(
            flops=steps * 2 * 5 * 200, bytes_accessed=8 * chunks * length * 64, transcendentals=steps
        ),
        name="attend_backward",
    )(*sources, lse)


def split_kernel(me_ref, source_ref, *out_refs, heads):
    turn = pl.program_id(0)
    for k in range(len(out_refs) // heads):

        @pl.when(turn == k)
        def _():
            for j in range(heads):
                out_refs[k * heads + j][...] = source_ref[0, j]


def split(values, me):
    chunks, heads, height, count = values.shape
    outs = pl.pallas_call(
        functools.partial(split_kernel, heads=heads),
        grid_spec=pltpu.PrefetchScalarGridSpec(
            num_scalar_prefetch=1,
            grid=(chunks,),
            in_specs=[pl.BlockSpec((1, heads, height, count), lambda k, m: (m[0] ^ k, 0, 0, 0))],
            out_specs=[fixed((height, count))] * (chunks * heads),
        ),
        out_shape=[jax.ShapeDtypeStruct((height, count), bf16)] * (chunks * heads),
        compiler_params=pltpu.CompilerParams(vmem_limit_bytes=VMEM),
        cost_estimate=pl.CostEstimate(flops=0, bytes_accessed=4 * values.size, transcendentals=0),
        name="split",
    )(me, values)
    return [[outs[k * heads + j] for k in range(chunks)] for j in range(heads)]


def split_pair_kernel(me_ref, query_ref, keyval_ref, *out_refs, heads):
    turn = pl.program_id(0)
    places = Places(out_refs[0].shape, query_ref.shape[3])
    length = places.length
    for k in range(len(out_refs) // heads):

        @pl.when(turn == k)
        def _():
            for j in range(heads):
                out_ref = out_refs[k * heads + j]
                out_ref[places.query()] = query_ref[0, j]
                out_ref[places.keys(0, length)] = keyval_ref[0, j, :HD, :]
                out_ref[places.values(0, length)] = keyval_ref[0, j, HD:, :]


def split_pair(queries, keyvals, me):
    chunks, heads, _, count = queries.shape
    length = keyvals.shape[3]
    shape = (HD, count + 2 * length)
    outs = pl.pallas_call(
        functools.partial(split_pair_kernel, heads=heads),
        grid_spec=pltpu.PrefetchScalarGridSpec(
            num_scalar_prefetch=1,
            grid=(chunks,),
            in_specs=[
                pl.BlockSpec((1, heads, HD, count), lambda k, m: (m[0] ^ k, 0, 0, 0)),
                pl.BlockSpec((1, heads, 2 * HD, length), lambda k, m: (m[0] ^ k, 0, 0, 0)),
            ],
            out_specs=[fixed(shape)] * (chunks * heads),
        ),
        out_shape=[jax.ShapeDtypeStruct(shape, bf16)] * (chunks * heads),
        compiler_params=pltpu.CompilerParams(vmem_limit_bytes=VMEM),
        cost_estimate=pl.CostEstimate(
            flops=0, bytes_accessed=4 * (queries.size + keyvals.size), transcendentals=0
        ),
        name="split_pair",
    )(me, queries, keyvals)
    return [[outs[k * heads + j] for k in range(chunks)] for j in range(heads)]


def assemble_pair_kernel(me_ref, *refs, heads):
    turn = pl.program_id(0)
    refs, (query_ref, keyval_ref) = refs[:-2], refs[-2:]
    places = Places(refs[0].shape, query_ref.shape[3])
    length = places.length
    for k in range(len(refs) // heads):

        @pl.when(turn == k)
        def _():
            for j in range(heads):
                source = refs[k * heads + j]
                query_ref[0, j] = source[places.query()]
                keyval_ref[0, j, :HD, :] = source[places.keys(0, length)]
                keyval_ref[0, j, HD:, :] = source[places.values(0, length)]


def assemble_pair(parts, me, count):
    heads, chunks = len(parts), len(parts[0])
    shape = parts[0][0].shape
    length = (shape[1] - count) // 2
    sources = [parts[j][k] for k in range(chunks) for j in range(heads)]
    return pl.pallas_call(
        functools.partial(assemble_pair_kernel, heads=heads),
        grid_spec=pltpu.PrefetchScalarGridSpec(
            num_scalar_prefetch=1,
            grid=(chunks,),
            in_specs=[fixed(shape)] * (chunks * heads),
            out_specs=[
                pl.BlockSpec((1, heads, HD, count), lambda k, m: (m[0] ^ k, 0, 0, 0)),
                pl.BlockSpec((1, heads, 2 * HD, length), lambda k, m: (m[0] ^ k, 0, 0, 0)),
            ],
        ),
        out_shape=[
            jax.ShapeDtypeStruct((chunks, heads, HD, count), bf16),
            jax.ShapeDtypeStruct((chunks, heads, 2 * HD, length), bf16),
        ],
        compiler_params=pltpu.CompilerParams(vmem_limit_bytes=VMEM),
        cost_estimate=pl.CostEstimate(
            flops=0, bytes_accessed=4 * chunks * heads * HD * shape[1], transcendentals=0
        ),
        name="assemble_pair",
    )(me, *sources)


def assemble_kernel(me_ref, *refs, heads):
    turn = pl.program_id(0)
    out_ref = refs[-1]
    for k in range((len(refs) - 1) // heads):

        @pl.when(turn == k)
        def _():
            for j in range(heads):
                out_ref[0, j] = refs[k * heads + j][...]


def assemble(parts, me):
    heads, chunks = len(parts), len(parts[0])
    height, count = parts[0][0].shape
    sources = [parts[j][k] for k in range(chunks) for j in range(heads)]
    return pl.pallas_call(
        functools.partial(assemble_kernel, heads=heads),
        grid_spec=pltpu.PrefetchScalarGridSpec(
            num_scalar_prefetch=1,
            grid=(chunks,),
            in_specs=[fixed((height, count))] * (chunks * heads),
            out_specs=pl.BlockSpec((1, heads, height, count), lambda k, m: (m[0] ^ k, 0, 0, 0)),
        ),
        out_shape=jax.ShapeDtypeStruct((chunks, heads, height, count), bf16),
        compiler_params=pltpu.CompilerParams(vmem_limit_bytes=VMEM),
        cost_estimate=pl.CostEstimate(
            flops=0, bytes_accessed=4 * chunks * heads * height * count, transcendentals=0
        ),
        name="assemble",
    )(me, *sources)


def tap_rows(cell_ref, frac_ref, live, plane, points):
    cell = cell_ref[0, plane : plane + 1, points]
    row = cell // (2 * G)
    col = cell - row * (2 * G)
    across = frac_ref[0, 2 * plane : 2 * plane + 1, points]
    downward = frac_ref[0, 2 * plane + 1 : 2 * plane + 2, points]
    half = lax.broadcasted_iota(jnp.int32, (G, cell.shape[1]), 0) * 2

    def spread(start, fraction, odd, gate):
        place = half + odd
        return jnp.where(
            place == start,
            (1.0 - fraction) * gate,
            jnp.where(place == start + 1, fraction * gate, 0.0),
        )

    return (
        [spread(row, downward, odd, live) for odd in range(2)],
        [spread(col, across, odd, 1.0) for odd in range(2)],
    )


def tap_table(table_ref, down, side):
    for ty in range(G):
        table_ref[ty * G : (ty + 1) * G, :] = lower(down[ty : ty + 1, :] * side)


def sample_kernel(
    object_ref, cell_ref, frac_ref, live_ref, chunk_ref, out_ref, table_ref, picked_ref, plane_ref, *, width
):
    turn = pl.program_id(1)

    @pl.when(turn == 0)
    def _():
        chunks = chunk_ref.shape[1]
        rows = TOK_OBJ // (2 * chunks)
        for r in range(chunks):
            for s in range(2):
                start = (s * chunks + r) * rows
                plane_ref[:, start : start + rows] = chunk_ref[0, r, :, s * rows : (s + 1) * rows]

    lanes = pl.ds(pl.multiple_of(turn * width, width), width)
    live = jnp.concatenate([live_ref[0]] * (width // RB), axis=1)
    picked = jnp.zeros((CH, width), f32)
    slot = 0
    for plane in range(3):
        downs, sides = tap_rows(cell_ref, frac_ref, live, plane, lanes)
        for dy in range(2):
            for dx in range(2):
                tap_table(table_ref.at[slot], downs[dy], sides[dx])
                part = (2 * dy + dx) * CH
                features = plane_ref[part : part + CH, plane * PIX : (plane + 1) * PIX]
                picked = picked + dot(features, table_ref[slot], NN)
                slot = 1 - slot
    picked_ref[:, lanes] = picked

    @pl.when(turn == pl.num_programs(1) - 1)
    def _():
        for s in range(out_ref.shape[1] // CH):
            out_ref[:, s * CH : (s + 1) * CH] = lower(picked_ref[:, s * RB : (s + 1) * RB].T)


def sample_points(planes, owner, cells, fractions, live):
    points = cells.shape[2]
    width = 512
    out = (RB, points // RB * CH)
    return pl.pallas_call(
        functools.partial(sample_kernel, width=width),
        grid_spec=pltpu.PrefetchScalarGridSpec(
            num_scalar_prefetch=1,
            grid=(1, points // width),
            in_specs=[
                fixed((1, 3, points)),
                fixed((1, 6, points)),
                fixed((1, 1, RB)),
                pl.BlockSpec((1,) + planes.shape[1:], lambda b, t, o: (o[b], 0, 0, 0)),
            ],
            out_specs=fixed(out),
            scratch_shapes=[
                pltpu.VMEM((2, PIX, width), bf16),
                pltpu.VMEM((CH, points), f32),
                pltpu.VMEM((4 * CH, TOK_OBJ), bf16),
            ],
        ),
        out_shape=jax.ShapeDtypeStruct(out, bf16),
        compiler_params=pltpu.CompilerParams(vmem_limit_bytes=VMEM),
        cost_estimate=pl.CostEstimate(
            flops=points * 3 * 4096 * 2 * 256, bytes_accessed=5 * 2**20, transcendentals=0
        ),
        name="sample_points",
    )(owner, cells, fractions, live, planes)


def scatter_kernel(object_ref, cell_ref, frac_ref, live_ref, grad_ref, out_ref, table_ref, rows_ref, total_ref, *, width):
    block = pl.program_id(0)
    turn = pl.program_id(1)
    owner = object_ref[block]

    @pl.when((block == 0) & (turn == 0))
    def _():
        total_ref[...] = jnp.zeros_like(total_ref)

    @pl.when(turn == 0)
    def _():
        for s in range(SAMP):
            rows_ref[:, s * RB : (s + 1) * RB] = grad_ref[:, s * CH : (s + 1) * CH].T

    lanes = pl.ds(pl.multiple_of(turn * width, width), width)
    live = jnp.concatenate([live_ref[0]] * (width // RB), axis=1)
    grads = rows_ref[:, lanes]
    slot = 0
    for plane in range(3):
        downs, sides = tap_rows(cell_ref, frac_ref, live, plane, lanes)
        for dy in range(2):
            for dx in range(2):
                tap_table(table_ref.at[slot], downs[dy], sides[dx])
                part = (2 * dy + dx) * CH
                total_ref[owner, part : part + CH, plane * PIX : (plane + 1) * PIX] += dot(
                    grads, table_ref[slot], NT
                )
                slot = 1 - slot

    @pl.when((block == pl.num_programs(0) - 1) & (turn == pl.num_programs(1) - 1))
    def _():
        objects, chunks = out_ref.shape[:2]
        rows = TOK_OBJ // (2 * chunks)
        for o in range(objects):
            for r in range(chunks):
                for s in range(2):
                    start = (s * chunks + r) * rows
                    out_ref[o, r, :, s * rows : (s + 1) * rows] = lower(
                        total_ref[o, :, start : start + rows]
                    )


def scatter_points(grads, owners, cells, fractions, live, objects, chunks):
    blocks = owners.shape[0]
    points = RB * SAMP
    width = 512
    shape = (objects, 4 * CH, TOK_OBJ)
    spread = (objects, chunks, 4 * CH, TOK_OBJ // chunks)
    return pl.pallas_call(
        functools.partial(scatter_kernel, width=width),
        grid_spec=pltpu.PrefetchScalarGridSpec(
            num_scalar_prefetch=1,
            grid=(blocks, points // width),
            in_specs=[
                pl.BlockSpec((1, 3, points), lambda b, t, o: (b, 0, 0)),
                pl.BlockSpec((1, 6, points), lambda b, t, o: (b, 0, 0)),
                pl.BlockSpec((1, 1, RB), lambda b, t, o: (b, 0, 0)),
                pl.BlockSpec((RB, SAMP * CH), lambda b, t, o: (b, 0)),
            ],
            out_specs=fixed(spread),
            scratch_shapes=[
                pltpu.VMEM((2, PIX, width), bf16),
                pltpu.VMEM((CH, points), bf16),
                pltpu.VMEM(shape, f32),
            ],
        ),
        out_shape=jax.ShapeDtypeStruct(spread, bf16),
        compiler_params=pltpu.CompilerParams(vmem_limit_bytes=VMEM),
        cost_estimate=pl.CostEstimate(
            flops=blocks * points * 3 * 4096 * 2 * 256,
            bytes_accessed=blocks * 5 * 2**20,
            transcendentals=0,
        ),
        name="scatter_points",
    )(owners, cells, fractions, live, grads)


SWAP = [(0, 1), (1, 0)]


def body(
    dp_axes,
    group_axes,
    tokens,
    dino,
    first_gain,
    first_shift,
    image_weight,
    cross_query,
    cross_keyval,
    cross_output,
    second_gain,
    second_shift,
    self_project,
    self_output,
    third_gain,
    third_shift,
    hidden_weight,
    hidden_bias,
    output_weight,
    deconv_weight,
    ray_mask,
    block_object,
    sample_cell,
    sample_frac,
    out_grad,
    sampled_grad,
):
    shard_axes = ("h",) + group_axes
    every = dp_axes + shard_axes
    outer, core = dp_axes
    group = 2 ** len(group_axes)
    heads = H // group
    half = lax.axis_index("h")
    side = lax.axis_index(core)
    over = lax.axis_index(outer)
    place = lax.axis_index(group_axes)
    me = place.reshape(1).astype(jnp.int32)
    rows = tokens.shape[0]
    count = 2 * rows
    patches = 2 * dino.shape[0]
    share = first_gain.shape[0]
    join = lax.optimization_barrier

    def own_object(values):
        mine = lax.dynamic_index_in_dim(values, half, 1, keepdims=False)
        other = lax.dynamic_index_in_dim(values, 1 - half, 1, keepdims=False)
        got = lax.ppermute(other, "h", SWAP)
        return jnp.concatenate(
            [jnp.where(half == 0, mine, got), jnp.where(half == 0, got, mine)], axis=0
        )

    def gather(pieces):
        return lax.all_gather(jnp.concatenate(pieces, axis=1), every, axis=0, tiled=True)

    def exchange(chunks):
        return [chunks[0]] + [
            lax.ppermute(chunks[k], group_axes, [(i, i ^ k) for i in range(group)])
            for k in range(1, group)
        ]

    def after(values, *other):
        return join((values, other))[0]

    def in_turn(call, *lists):
        done = []
        for operands in zip(*lists):
            done.append(call(*(after(operands, done[-1]) if done else operands)))
        return done

    def exchange_all(parts):
        done = []
        for chunks in parts:
            if done:
                chunks, done[-1] = join((chunks, done[-1]))
            done.append(exchange(chunks))
        return done

    columns = jnp.stack(
        [first_gain, first_shift, second_gain, second_shift, third_gain, third_shift], axis=1
    )
    columns = jnp.concatenate([columns, hidden_bias.reshape(share, FF // D)], axis=1)
    columns = jnp.pad(columns, ((0, 0), (0, 128 - columns.shape[1])))
    early = gather(
        [
            lower(cross_query),
            lower(cross_keyval),
            lower(image_weight).reshape(share, DINO),
            lower(columns),
        ]
    )
    query_w = early[:, :D]
    keyval_w = early[:, D : 3 * D]
    image_w = early[:, 3 * D : 3 * D + DINO].reshape(DINO, D)
    vectors = widen(early[:, 3 * D + DINO :])
    gain_a, shift_a, gain_b, shift_b, gain_c, shift_c = [vectors[:, i] for i in range(6)]
    bias = vectors[:, 6 : 6 + FF // D].reshape(FF)

    blocks = ray_mask.shape[0] // RB

    def by_sample(values):
        kinds = values.shape[0]
        values = values.reshape(kinds, blocks, RB, SAMP)
        return values.transpose(1, 0, 3, 2).reshape(blocks, kinds, SAMP * RB)

    cells = by_sample(sample_cell)
    fractions = by_sample(sample_frac)
    live = widen(ray_mask).reshape(blocks, 1, RB)
    plane_grad = scatter_points(sampled_grad, block_object, cells, fractions, live, 2, group)
    token_low = own_object(tokens)
    dino_values = own_object(dino)
    plane_grad, token_low, dino_values = join((plane_grad, token_low, dino_values))
    token_values = widen(token_low)

    normed_full, unit_a, inverse_a = normalize(token_values, gain_a, shift_a)
    normed_a = lower(normed_full)
    image = lower(dot(dino_values, image_w, NN))
    queries = lower(dot(query_w, normed_a, ((0,), (1,)))).reshape(group, heads, HD, count)
    keyvals = lower(dot(keyval_w, image, ((0,), (1,)))).reshape(group, heads, 2 * HD, patches)
    cross_in = exchange_all(split_pair(queries, keyvals, me))
    middle = [lower(cross_output), lower(self_project), lower(self_output)]
    late = [lower(hidden_weight), lower(deconv_weight)]
    output_w = lower(output_weight)
    plane_grad = after(plane_grad, cross_in[0])
    plane_low = lax.psum_scatter(
        plane_grad.reshape(2 * group * 4 * CH, count), shard_axes, scatter_dimension=0, tiled=True
    )
    middle, late = gather(middle), gather(late)
    output_w = lax.all_gather(output_w, every, axis=0, tiled=True)
    cross_w = middle[:, :D]
    project_w = middle[:, D : 4 * D]
    self_w = middle[:, 4 * D :]
    hidden_w = late[:, :FF]
    deconv_w = late[:, FF:]
    cross_out = in_turn(lambda x: attend_forward(x, count), cross_in)
    cross_mix = assemble([exchange(o) for o, _ in cross_out], me).reshape(D, count)
    after_cross = token_values + dot(cross_mix, cross_w, TN)

    normed_full, unit_b, inverse_b = normalize(after_cross, gain_b, shift_b)
    normed_b = lower(normed_full)
    projected = lower(dot(project_w, normed_b, ((0,), (1,)))).reshape(group, heads, 3 * HD, count)
    projected, out_grad = join((split(projected, me), out_grad))
    out_cotangent = own_object(out_grad)
    self_qkv = exchange_all(projected)
    self_out = in_turn(lambda x: attend_forward(x, count), self_qkv)
    out_cotangent = after(out_cotangent, self_out[-1])
    self_mix = assemble([exchange(o) for o, _ in self_out], me).reshape(D, count)
    after_self = after_cross + dot(self_mix, self_w, TN)

    normed_full, unit_c, inverse_c = normalize(after_self, gain_c, shift_c)
    normed_c = lower(normed_full)
    hidden = dot(normed_c, hidden_w, NN) + bias
    activated = lower(gelu(hidden))
    result_low = lower(after_self + dot(activated, output_w, NN))

    planes = lower(dot(deconv_w, result_low, ((0,), (1,))))
    plane_all = lax.all_gather(planes, shard_axes, axis=0, tiled=True)
    plane_all = plane_all.reshape(2, group, 4 * CH, count)


    def grad_job(left, axis, right, right_axis, pieces=1):
        quarter = left.shape[axis] // 4
        dims = ((1 - axis,), (right_axis,))

        def block(y, c):
            part = lax.dynamic_slice_in_dim(left, (2 * y + c) * quarter, quarter, axis)
            return dot(part, right, dims)

        others = [lower(block(y, 1 - side)) for y in (1 - over, over)]
        others = yield (), [(x, core) for x in others]
        away = lower(block(1 - over, side) + widen(others[0]))
        kept = lower(block(over, side) + widen(others[1]))
        width = away.shape[1] // pieces
        got = []
        for i in range(pieces):
            got += yield kept, [(away[:, i * width : (i + 1) * width], outer)]
        return lower(widen(kept) + widen(jnp.concatenate(got, axis=1) if pieces > 1 else got[0]))

    def chain_job(values):
        left = list(shard_axes)
        values = [v.reshape((2,) * len(left) + (-1, v.shape[-1])) for v in values]
        for axis in group_axes[::-1] + ("h",):
            dim, here = left.index(axis), lax.axis_index(axis)
            left.pop(dim)
            away = [lax.dynamic_index_in_dim(v, 1 - here, dim, keepdims=False) for v in values]
            kept = [lax.dynamic_index_in_dim(v, here, dim, keepdims=False) for v in values]
            got = yield kept, [(x, axis) for x in away]
            values = [widen(k) + widen(g) for k, g in zip(kept, got)]
            if left:
                values = [lower(v) for v in values]
        return values

    def full_job(*args):
        part = yield from grad_job(*args)
        return (yield from chain_job([part]))[0]

    def swap_job(arrays, pieces):
        done = []
        for values in arrays:
            size = values.shape[0] // 2
            step = size // pieces
            mine = lax.dynamic_slice_in_dim(values, half * size, size, 0)
            away = lower(lax.dynamic_slice_in_dim(values, (1 - half) * size, size, 0))
            got = []
            for i in range(pieces):
                got += yield done, [(away[i * step : (i + 1) * step], "h")]
            got = jnp.concatenate(got, axis=0).astype(mine.dtype)
            done.append(
                jnp.stack([jnp.where(half == 0, mine, got), jnp.where(half == 0, got, mine)], axis=1)
            )
        return done

    jobs, sums_of = {}, {}

    def turn(call, operands):
        kept, sent = {}, {}
        for name in list(jobs):
            job, got = jobs[name]
            try:
                kept[name], sent[name] = next(job) if got is None else job.send(got)
            except StopIteration as end:
                sums_of[name] = end.value
                del jobs[name]
        arrays = {name: [x for x, _ in sent[name]] for name in sent}
        operands, arrays, _ = join((operands, arrays, kept))
        moved = {
            name: [lax.ppermute(x, axis, SWAP) for x, (_, axis) in zip(arrays[name], sent[name])]
            for name in sent
        }
        raw = call(*operands)
        moved, settled = join((moved, raw))
        for name in sent:
            jobs[name] = (jobs[name][0], moved[name])
        return raw, settled

    def start(name, job):
        jobs[name] = (job, None)

    result_grad = widen(out_cotangent) + dot(plane_low, deconv_w, ((0,), (1,)))
    result_low_grad = lower(result_grad)
    activated_grad = dot(result_low_grad, output_w, NT)
    _, gelu_pull = jax.vjp(gelu, hidden)
    hidden_grad = lower(gelu_pull(activated_grad)[0])
    bias_grad = jnp.sum(widen(hidden_grad), axis=0)
    back_c, gain_c_grad, shift_c_grad = normalize_back(
        dot(hidden_grad, hidden_w, NT), unit_c, inverse_c, gain_c
    )
    self_grad = result_grad + back_c

    self_low = lower(self_grad)
    self_mix_grad = lower(dot(self_w, self_low, NT)).reshape(group, heads, HD, count)
    self_dout = exchange_all(split(self_mix_grad, me))
    start("output", full_job(activated, 1, result_low_grad, 0, 2))
    gone = ()
    self_back = []
    for j in range(heads):
        if j == min(2, heads - 1):
            start("hidden", full_job(normed_c, 1, hidden_grad, 0, 2))
            start("self", full_job(self_mix, 0, self_low, 0, 1))
            start("deconv", full_job(result_low, 1, plane_low, 1, 1))
        if j == min(1, heads - 1):
            start("tokens_out", swap_job([result_low], 4))
        raw, gone = turn(
            lambda s, g, o: attend_backward(s, g, *o),
            (after(self_qkv[j], gone), self_dout[j], self_out[j]),
        )
        self_back.append(raw)

    project_grad = assemble([exchange(g) for g in self_back], me).reshape(3 * D, count)
    back_b, gain_b_grad, shift_b_grad = normalize_back(
        dot(project_grad, project_w, ((0,), (1,))), unit_b, inverse_b, gain_b
    )
    cross_grad = self_grad + back_b

    cross_low = lower(cross_grad)
    cross_mix_grad = lower(dot(cross_w, cross_low, NT)).reshape(group, heads, HD, count)
    cross_dout = exchange_all(split(cross_mix_grad, me))
    start("project", full_job(normed_b, 1, project_grad, 1, 2))
    start("cross", full_job(cross_mix, 0, cross_low, 0, 1))
    cut = heads // 2
    cross_back, parts, found = [], [], []

    def kv_grads(first, last):
        queries, keyvals = assemble_pair(parts[first:last], me, count)
        queries = queries.reshape(-1, count)
        keyvals = keyvals.reshape(-1, patches)
        start(f"keyval{first}", grad_job(image, 1, keyvals, 1))
        start(f"query{first}", grad_job(normed_a, 1, queries, 1))
        found.append((queries, keyvals))

    for j in range(heads):
        if cut and j == cut + 1:
            parts[:cut] = after(parts[:cut], gone)
            kv_grads(0, cut)
        raw, gone = turn(
            lambda s, g, o: attend_backward(s, g, *o),
            (after(cross_in[j], gone), cross_dout[j], cross_out[j]),
        )
        cross_back.append(raw)
        parts.append(exchange(raw))

    pieces = [(b, s) for b in range(blocks) for s in range(2)]
    span = SAMP * RB // 2
    sampled = {}

    def sample_turn(gone):
        b, s = pieces[len(sampled)]
        operands = (
            plane_all,
            block_object[b : b + 1],
            cells[b : b + 1, :, s * span : (s + 1) * span],
            fractions[b : b + 1, :, s * span : (s + 1) * span],
            live[b : b + 1],
        )
        _, sampled[b, s] = turn(sample_points, after(operands, gone))
        return sampled[b, s]

    gone = sample_turn(gone)
    parts[cut:] = after(parts[cut:], gone)
    kv_grads(cut, heads)

    def merge(pieces, height):
        folded = [p.reshape(group, -1, height, p.shape[-1]) for p in pieces]
        return jnp.concatenate(folded, axis=1).reshape(-1, pieces[0].shape[-1])

    def merge_columns(pieces, height):
        folded = [p.reshape(p.shape[0], group, -1, height) for p in pieces]
        return jnp.concatenate(folded, axis=2).reshape(pieces[0].shape[0], -1)

    query_back = merge([f[0] for f in found], HD)
    keyval_back = merge([f[1] for f in found], 2 * HD)
    image_grad = lower(dot(keyval_back, keyval_w, ((0,), (1,))))
    start("image", grad_job(dino_values, 1, image_grad, 0))
    back_a, gain_a_grad, shift_a_grad = normalize_back(
        dot(query_back, query_w, ((0,), (1,))), unit_a, inverse_a, gain_a
    )
    dino_grad = dot(image_grad, image_w, NT)
    tokens_grad = cross_grad + back_a

    sums = jnp.stack(
        [gain_a_grad, shift_a_grad, gain_b_grad, shift_b_grad, gain_c_grad, shift_c_grad], axis=1
    )
    sums = jnp.concatenate([sums, bias_grad.reshape(D, FF // D)], axis=1)
    sums = jnp.pad(sums, ((0, 0), (0, 128 - sums.shape[1])))

    def vector_job():
        def quarter_rows(y, c):
            return lax.dynamic_slice_in_dim(sums, (2 * y + c) * (D // 4), D // 4, 0)

        others = yield (), [(quarter_rows(y, 1 - side), core) for y in (1 - over, over)]
        away = quarter_rows(1 - over, side) + others[0]
        kept = quarter_rows(over, side) + others[1]
        got = yield kept, [(away, outer)]
        return lower(kept + got[0])

    start("vectors", vector_job())
    (dino_grad, tokens_grad), gone = join(((dino_grad, tokens_grad), gone))
    start("swap", swap_job([dino_grad, tokens_grad], 2))
    gone = sample_turn(gone)
    gone = sample_turn(gone)
    names = [f"{kind}{at}" for at in ([0, cut] if cut else [0]) for kind in ("keyval", "query")]
    names += ["vectors", "image"]
    while any(name in jobs for name in names):
        _, gone = turn(lambda *x: x, (gone,))
    last_part = jnp.concatenate([sums_of[name] for name in names[:-1]], axis=1)
    start("last", chain_job([last_part, sums_of["image"]]))
    gone = sample_turn(gone)
    while jobs:
        _, gone = turn(lambda *x: x, (gone,))
    last, image_sum = sums_of["last"]
    dino_grad, tokens_grad = sums_of["swap"]
    (tokens_out,) = sums_of["tokens_out"]
    sampled = jnp.concatenate(
        [jnp.concatenate([sampled[b, s] for s in range(2)], axis=1) for b in range(blocks)], axis=0
    )

    keyval_sums, query_sums = [], []
    at = 0
    for width in [group * n * HD for n in ([cut, heads - cut] if cut else [heads])]:
        keyval_sums.append(last[:, at : at + 2 * width])
        query_sums.append(last[:, at + 2 * width : at + 3 * width])
        at += 3 * width
    vector_sums = last[:, at:]

    return (
        tokens_out,
        sampled,
        tokens_grad,
        dino_grad,
        vector_sums[:, 0],
        vector_sums[:, 1],
        image_sum,
        merge_columns(query_sums, HD),
        merge_columns(keyval_sums, 2 * HD),
        sums_of["cross"],
        vector_sums[:, 2],
        vector_sums[:, 3],
        sums_of["project"],
        sums_of["self"],
        vector_sums[:, 4],
        vector_sums[:, 5],
        sums_of["hidden"],
        vector_sums[:, 6 : 6 + FF // D].reshape(share * (FF // D)),
        sums_of["output"],
        sums_of["deconv"],
    )


def solution(mesh):
    dp_bits = mesh.shape["dp"].bit_length() - 1
    shard_bits = mesh.shape["shard"].bit_length() - 1
    dp_axes = tuple(f"d{i}" for i in range(dp_bits))
    group_axes = tuple(f"r{i}" for i in range(shard_bits - 1))
    shard_axes = ("h",) + group_axes
    fine = Mesh(mesh.devices.reshape((2,) * (dp_bits + shard_bits)), dp_axes + shard_axes)
    every = dp_axes + shard_axes
    rows = P(shard_axes, dp_axes, None)
    vector = P(every)
    matrix = P(every, None)
    points = P(None, every)
    return jax.shard_map(
        functools.partial(body, dp_axes, group_axes),
        mesh=fine,
        in_specs=(
            rows, rows,
            vector, vector, matrix, matrix, matrix, matrix,
            vector, vector, matrix, matrix,
            vector, vector, matrix, vector, matrix, matrix,
            vector, vector, points, points, rows, matrix,
        ),
        out_specs=(
            rows, matrix, rows, rows,
            vector, vector, matrix, matrix, matrix, matrix,
            vector, vector, matrix, matrix,
            vector, vector, matrix, vector, matrix, matrix,
        ),
        check_vma=False,
    )
```
